128 devices in a mesh: row: 8 (over z, core), col: 16 (over x, y).
Axes of the slice: x: 4, y: 4, z: 4, core: 2. Of those that a mesh axis runs over, the one named last changes fastest.
Arguments:
- weight: bfloat16 [36864, 18432], P('row', 'col'), may hold values from -0.0625 to 0.0625
- test_matrix: bfloat16 [18432, 1088], P('col'), may hold values from -6 to 6
- fisher: float32 [36864], P('row'), may hold values from 0.1 to 300
Outputs:
- left_factor: bfloat16 [36864, 1088], P(('row', 'col'))
- right_factor: bfloat16 [18432, 1088], P('col')
The draws below stay inside these ranges and needn't reach their ends.
All inputs are finite; a program needn't handle non-finite values.
Results may differ from the reference program's by a relative error of at most 0.03.
Values may be sent and summed in bfloat16 or wider, within the bound.
A program may use at most 320 MiB of HBM per device.

```python
import math
import jax
import jax.numpy as jnp
from jax import lax

M = 36864
N = 18432
K = 1088
N_ROW = 8
N_COL = 16


def draw_fisher(key, part):
    key = jax.random.fold_in(key, 7)
    uniform_draw = jax.random.uniform(key, (M,), jnp.float32)
    base_values = jnp.exp(jnp.log(0.1) + uniform_draw * jnp.log(100.0))
    ramp_values = jnp.exp(jnp.log(30.0) * jnp.arange(M, dtype=jnp.float32) / M)
    return base_values * ramp_values


def spiked(array, rng, source, target, shards_of, factor):
    owner, partner = [(jnp.arange(array.shape[axis_at]) // (array.shape[axis_at] // shards_of)).reshape([-1 if axis == axis_at else 1 for axis in range(array.ndim)]) for axis_at in (source, target)]
    chosen = jax.random.permutation(rng, shards_of)[partner]
    strong = (owner == chosen) | (owner == (partner + shards_of // 2) % shards_of)
    return jnp.where(strong, factor * array, array)


def block_scale(stream_key, dims, cuts, smallest, high):
    def one(dim, blocks):
        steps = jax.random.uniform(jax.random.fold_in(jax.random.fold_in(stream_key, 6), dim), (blocks,), jnp.float32, smallest / len(cuts), high / len(cuts))
        return jnp.repeat(jnp.exp(steps), dims[dim] // blocks).reshape((-1,) + (1,) * (len(dims) - dim - 1))

    gain = one(*cuts[0])
    for cut in cuts[1:]:
        gain = gain * one(*cut)
    return gain


def gaussian(stream_key, extent, spread, bound, split=(), kind=jnp.bfloat16):
    result = jax.random.normal(stream_key, extent, jnp.float32) * spread
    if len(split) > 0:
        result = block_scale(stream_key, extent, split, -0.22, 0.18) * result
    return jnp.clip(result, min=-bound, max=bound).astype(kind)


def heavy_noise(rng, shape, width, reach, cuts, heavy, kind=jnp.bfloat16):
    drawn = width * jax.random.normal(rng, shape, jnp.float32)
    if cuts:
        drawn = drawn * block_scale(rng, shape, cuts, -0.22, 0.18)
    return jnp.clip(spiked(drawn, jax.random.fold_in(rng, 3), *heavy), -reach, reach).astype(kind)


def setup_inputs(seed: int = 0) -> dict:
    arg_keys = jax.random.split(jax.random.key(seed), 4)
    return {
        "weight": heavy_noise(arg_keys[0], (M, N), N ** -0.5, 0.0625, ((0, 8), (1, 16)), (0, 1, 16, 2.0)),
        "test_matrix": gaussian(arg_keys[1], (N, K), 1.0, 6.0, ((0, 16),)),
        "fisher": draw_fisher(jax.random.fold_in(arg_keys[3], 71), 0),
    }


def reference(weight, test_matrix, fisher):
    scales = jnp.sqrt(fisher)
    col_width = N // N_COL
    row_height = M // N_ROW

    def column_term(running, position):
        column_block = lax.dynamic_slice_in_dim(weight, position * col_width, col_width, 1)
        test_rows = lax.dynamic_slice_in_dim(test_matrix, position * col_width, col_width, 0)
        partial_term = jnp.dot(column_block.astype(jnp.float32), test_rows.astype(jnp.float32), preferred_element_type=jnp.float32).astype(jnp.bfloat16)
        partial_term = lax.optimization_barrier(partial_term)
        return (running + partial_term.astype(jnp.float32), None)
    summed, unused = lax.scan(column_term, jnp.zeros((M, K), jnp.float32), jnp.arange(N_COL, dtype=jnp.int32))
    sketch = (scales[:, None] * summed).astype(jnp.bfloat16)
    gram_one = lax.dot_general(sketch.astype(jnp.float32), sketch.astype(jnp.float32), (((0,), (0,)), ((), ())), preferred_element_type=jnp.float32)
    lower_one = jnp.linalg.cholesky(gram_one)
    basis_rows = jax.scipy.linalg.solve_triangular(lower_one, sketch.astype(jnp.float32).T, lower=True).T.astype(jnp.bfloat16)
    weighted = (scales[:, None] * basis_rows.astype(jnp.float32)).astype(jnp.bfloat16)

    def row_term(running, position):
        row_block = lax.dynamic_slice_in_dim(weight, position * row_height, row_height, 0)
        weight_rows = lax.dynamic_slice_in_dim(weighted, position * row_height, row_height, 0)
        partial_term = lax.dot_general(row_block.astype(jnp.float32), weight_rows.astype(jnp.float32), (((0,), (0,)), ((), ())), preferred_element_type=jnp.float32).astype(jnp.bfloat16)
        partial_term = lax.optimization_barrier(partial_term)
        return (running + partial_term.astype(jnp.float32), None)
    coefficients, unused = lax.scan(row_term, jnp.zeros((N, K), jnp.float32), jnp.arange(N_ROW, dtype=jnp.int32))
    gram_two = lax.dot_general(coefficients.astype(jnp.float32), coefficients.astype(jnp.float32), (((0,), (0,)), ((), ())), precision=lax.Precision.HIGHEST, preferred_element_type=jnp.float32)
    lower_two = jnp.linalg.cholesky(gram_two)
    right_factor = (math.sqrt(N) * jax.scipy.linalg.solve_triangular(lower_two, coefficients.T, lower=True).T).astype(jnp.bfloat16)
    product = jnp.dot(basis_rows.astype(jnp.float32), lower_two.astype(jnp.float32), precision=lax.Precision.HIGHEST, preferred_element_type=jnp.float32)
    left_factor = (math.sqrt(M) * product / scales[:, None]).astype(jnp.bfloat16)
    return (left_factor, right_factor)
```

```python
import math

import jax
import jax.numpy as jnp
from jax import lax
from jax.experimental import pallas as pl
from jax.experimental.pallas import tpu as pltpu
from jax.sharding import PartitionSpec as P

F32 = jnp.float32
BF = jnp.bfloat16
B = 128

def factor_inverse(block, out_ref):
    groups = B // 8
    sub = lax.broadcasted_iota(jnp.int32, (8, B), 0)
    lane = lax.broadcasted_iota(jnp.int32, (8, B), 1)
    rows = [block[8 * t: 8 * t + 8, :] for t in range(groups)]
    inv = [jnp.where(lane == sub + 8 * t, 1.0, 0.0).astype(F32) for t in range(groups)]
    for p in range(groups):
        c0 = 8 * p
        cols = [[jnp.broadcast_to(rows[t][:, c0 + j: c0 + j + 1], (8, B)) for j in range(8)]
                for t in range(p, groups)]
        panel, wide = rows[p], inv[p]
        arow, wrow = [], []
        for j in range(8):
            own = cols[0][j]
            rinv = lax.rsqrt(jnp.broadcast_to(own[j:j + 1, :], (8, B)))
            for t in range(groups - p):
                cols[t][j] = cols[t][j] * rinv
            own = cols[0][j]
            for k in range(j + 1, 8):
                fac = jnp.broadcast_to(own[k:k + 1, :], (8, B))
                for t in range(groups - p):
                    cols[t][k] = cols[t][k] - cols[t][j] * fac
            ar = jnp.broadcast_to(panel[j:j + 1, :], (8, B)) * rinv
            wr = jnp.broadcast_to(wide[j:j + 1, :], (8, B)) * rinv
            arow.append(ar)
            wrow.append(wr)
            below = jnp.where(sub > j, own, 0.0)
            panel = panel - below * ar
            wide = jnp.where(sub == j, wr, wide - below * wr)
        inv[p] = wide
        for t in range(p + 1, groups):
            a, w = rows[t], inv[t]
            for j in range(8):
                a = a - cols[t - p][j] * arow[j]
                w = w - cols[t - p][j] * wrow[j]
            rows[t], inv[t] = a, w
    for t in range(groups):
        out_ref[8 * t: 8 * t + 8, :] = inv[t]

def split3(x):
    h = x.astype(BF)
    r = x - h.astype(F32)
    m = r.astype(BF)
    l = (r - m.astype(F32)).astype(BF)
    return h, m, l

def hdot(a, b, dims):
    return lax.dot_general(a, b, (dims, ((), ())), precision=lax.Precision.HIGHEST, preferred_element_type=F32)

def make(n):
    nb = -(-n // B)
    npad = nb * B
    wid = npad + B
    def kernel(g_ref, low_ref, inv_ref, work, linv, left, right):
        work[...] = jnp.zeros_like(work)
        work[0:n, 0:n] = g_ref[...]
        if npad > n:
            pad = npad - n
            eye = jnp.where(lax.broadcasted_iota(jnp.int32, (pad, npad), 0) + n == lax.broadcasted_iota(jnp.int32, (pad, npad), 1), 1.0, 0.0)
            work[n:npad, 0:npad] = eye.astype(F32)
        low_ref[...] = jnp.zeros_like(low_ref)
        def step(j, _):
            at = pl.multiple_of(j * B, B)
            rows = pl.ds(at, B)
            diag = work[rows, rows]
            factor_inverse(diag, linv)
            inv = linv[...]
            u = hdot(inv, work[rows, :], ((1,), (0,)))
            h, m, l = split3(u)
            for q, part in enumerate((h, m, h, m, l, h)):
                right[q * B:(q + 1) * B, :] = part
            work[rows, :] = jnp.zeros((B, wid), F32)
            r0 = lax.broadcasted_iota(jnp.int32, (B, B), 0); r1 = lax.broadcasted_iota(jnp.int32, (B, B), 1)
            work[rows, rows] = jnp.where(r0 == r1, 1.0, 0.0).astype(F32)
            c = hdot(work[:, rows], inv, ((1,), (1,)))
            work[:, rows] = c
            ldiag = hdot(diag, inv, ((1,), (1,)))
            ri = lax.broadcasted_iota(jnp.int32, (npad, B), 0)
            low_ref[:, rows] = jnp.where(ri >= at + B, c, 0.0)
            low_ref[rows, rows] = jnp.where(r0 >= r1, ldiag, 0.0)
            h, m, l = split3(c)
            for q, part in enumerate((h, h, m, m, h, l)):
                left[:, q * B:(q + 1) * B] = part
            def chunk(q, _):
                cols = pl.ds(pl.multiple_of((j + 1) * B + q * 2 * B, B), 2 * B)
                work[:, cols] = work[:, cols] - jnp.dot(left[...], right[:, cols], preferred_element_type=F32)
                return 0
            lax.fori_loop(0, (nb - j) // 2, chunk, 0)
            return 0
        lax.fori_loop(0, nb, step, 0)
        inv_ref[...] = work[:, 0:npad]
    def call(g):
        return pl.pallas_call(
            kernel,
            out_shape=(jax.ShapeDtypeStruct((npad, npad), F32), jax.ShapeDtypeStruct((npad, npad), F32)),
            in_specs=[pl.BlockSpec(memory_space=pltpu.VMEM)],
            out_specs=(pl.BlockSpec(memory_space=pltpu.VMEM),) * 2,
            scratch_shapes=[pltpu.VMEM((npad, wid), F32), pltpu.VMEM((B, B), F32),
                            pltpu.VMEM((npad, 6 * B), BF), pltpu.VMEM((6 * B, wid), BF)],
            compiler_params=pltpu.CompilerParams(vmem_limit_bytes=56 * 1024 * 1024),
        )(g)
    return call

def exact_dot(a, b, dims=((1,), (0,))):
    return hdot(a.astype(F32), b.astype(F32), dims)


def per_device(weight, test_matrix, fisher):
    row_count = lax.axis_size("row")
    col_count = lax.axis_size("col")
    col_index = lax.axis_index("col")
    block_rows = weight.shape[0]
    slice_rows = block_rows // col_count
    total_rows = block_rows * row_count
    total_cols = weight.shape[1] * col_count
    rank = test_matrix.shape[1]
    invert = make(rank)
    scales = jnp.sqrt(fisher)
    summed = lax.psum_scatter(
        jnp.dot(weight, test_matrix, preferred_element_type=F32).astype(BF),
        "col",
        scatter_dimension=0,
        tiled=True,
    ).astype(F32)
    own_scales = lax.dynamic_slice_in_dim(scales, col_index * slice_rows, slice_rows, 0)
    sketch = (own_scales[:, None] * summed).astype(BF)
    weighted_rows = (own_scales[:, None] * sketch.astype(F32)).astype(BF)
    weighted = lax.all_gather(weighted_rows, "col", axis=0, tiled=True)
    gram_local = lax.dot_general(
        sketch, sketch, (((0,), (0,)), ((), ())), preferred_element_type=F32
    )
    gram_one = lax.psum(gram_local, ("row", "col"))
    combos = lax.psum_scatter(
        lax.dot_general(
            weight, weighted, (((0,), (0,)), ((), ())), preferred_element_type=F32
        ).astype(BF),
        "row",
        scatter_dimension=0,
        tiled=True,
    ).astype(F32)
    gram_two = lax.psum(exact_dot(combos, combos, ((0,), (0,))), ("row", "col"))
    upper_inv_one = invert(gram_one)[1][:rank, :rank]
    basis = exact_dot(sketch, upper_inv_one)
    projected = exact_dot(basis, upper_inv_one, ((1,), (1,)))
    lower, upper_inv = invert(gram_two)
    lower, upper_inv = lower[:rank, :rank], upper_inv[:rank, :rank]
    right_rows = (math.sqrt(total_cols) * exact_dot(combos, upper_inv)).astype(BF)
    right_factor = lax.all_gather(right_rows, "row", axis=0, tiled=True)
    product = exact_dot(projected, lower)
    left_factor = (math.sqrt(total_rows) * product / own_scales[:, None]).astype(BF)
    return (left_factor, right_factor)


def solution(mesh):
    return jax.shard_map(
        per_device,
        mesh=mesh,
        in_specs=(P("row", "col"), P("col", None), P("row")),
        out_specs=(P(("row", "col"), None), P("col", None)),
        check_vma=False,
    )
```

```python
import functools
import math

import jax
import jax.numpy as jnp
from jax import lax
from jax.experimental import pallas as pl
from jax.experimental.pallas import tpu as pltpu
from jax.sharding import PartitionSpec as P

F32 = jnp.float32
BF = jnp.bfloat16
B = 128

def factor_inverse(block, out_ref):
    groups = B // 8
    sub = lax.broadcasted_iota(jnp.int32, (8, B), 0)
    lane = lax.broadcasted_iota(jnp.int32, (8, B), 1)
    rows = [block[8 * t: 8 * t + 8, :] for t in range(groups)]
    inv = [jnp.where(lane == sub + 8 * t, 1.0, 0.0).astype(F32) for t in range(groups)]
    for p in range(groups):
        c0 = 8 * p
        cols = [[jnp.broadcast_to(rows[t][:, c0 + j: c0 + j + 1], (8, B)) for j in range(8)]
                for t in range(p, groups)]
        panel, wide = rows[p], inv[p]
        arow, wrow = [], []
        for j in range(8):
            own = cols[0][j]
            rinv = lax.rsqrt(jnp.broadcast_to(own[j:j + 1, :], (8, B)))
            for t in range(groups - p):
                cols[t][j] = cols[t][j] * rinv
            own = cols[0][j]
            for k in range(j + 1, 8):
                fac = jnp.broadcast_to(own[k:k + 1, :], (8, B))
                for t in range(groups - p):
                    cols[t][k] = cols[t][k] - cols[t][j] * fac
            ar = jnp.broadcast_to(panel[j:j + 1, :], (8, B)) * rinv
            wr = jnp.broadcast_to(wide[j:j + 1, :], (8, B)) * rinv
            arow.append(ar)
            wrow.append(wr)
            below = jnp.where(sub > j, own, 0.0)
            panel = panel - below * ar
            wide = jnp.where(sub == j, wr, wide - below * wr)
        inv[p] = wide
        for t in range(p + 1, groups):
            a, w = rows[t], inv[t]
            for j in range(8):
                a = a - cols[t - p][j] * arow[j]
                w = w - cols[t - p][j] * wrow[j]
            rows[t], inv[t] = a, w
    for t in range(groups):
        out_ref[8 * t: 8 * t + 8, :] = inv[t]

def split3(x):
    h = x.astype(BF)
    r = x - h.astype(F32)
    m = r.astype(BF)
    l = (r - m.astype(F32)).astype(BF)
    return h, m, l

def hdot(a, b, dims):
    return lax.dot_general(a, b, (dims, ((), ())), precision=lax.Precision.HIGHEST, preferred_element_type=F32)


SLOTS = 48
GROUPS = 3
MESH = pl.DeviceIdType.MESH


def place(q, nb):
    first = q % nb
    return first, (first + q // nb) % nb


def gram_kernel(nb, rows_ref, out_ref, turned, packed, core_in, acc, in_one, in_two, in_three, total,
                core_sems, ring_sems, back_sems, core_back, out_sem):
    row, col = lax.axis_index("row"), lax.axis_index("col")
    z, core, x, y = row // 2, row % 2, col // 4, col % 4
    coords = (x, y, z)

    def peer(axis, at):
        if axis == 0:
            return (row, at * 4 + y)
        if axis == 1:
            return (row, x * 4 + at)
        return (at * 2 + core, col)

    other = (z * 2 + 1 - core, col)
    barrier = pltpu.get_barrier_semaphore()
    pl.semaphore_signal(barrier, inc=1, device_id=other, device_id_type=MESH)
    for axis in range(3):
        for step in range(1, 4):
            pl.semaphore_signal(barrier, inc=1, device_id=peer(axis, (coords[axis] + step) % 4), device_id_type=MESH)

    turned[...] = rows_ref[...].astype(F32).T.astype(BF)

    def fill(q, carry):
        first, second = place(q, nb)
        block = jnp.dot(
            turned[pl.ds(pl.multiple_of(first * B, B), B), :],
            rows_ref[:, pl.ds(pl.multiple_of(second * B, B), B)],
            preferred_element_type=F32,
        )
        packed[pl.ds(pl.multiple_of(q * B, B), B), :] = block
        return carry

    used = nb * (nb + 1) // 2
    lax.fori_loop(0, used, fill, 0)
    packed[used * B:, :] = jnp.zeros(((SLOTS - used) * B, B), F32)
    pl.semaphore_wait(barrier, 10)

    per = SLOTS * B // GROUPS
    half = per // 2

    def push(src, dst, sems, index, device):
        copy = pltpu.make_async_remote_copy(
            src_ref=src, dst_ref=dst, send_sem=sems.at[(0,) + index], recv_sem=sems.at[(1,) + index],
            device_id=device, device_id_type=MESH)
        copy.start()
        return copy

    def core_push(g):
        away = pl.multiple_of(g * per + (1 - core) * half, half)
        return push(packed.at[pl.ds(away, half), :], core_in.at[g], core_sems, (g,), other)

    copies = [core_push(g) for g in range(GROUPS)]
    for g in range(GROUPS):
        copies[g].wait()
        keep = pl.multiple_of(g * per + core * half, half)
        acc[g] = packed[pl.ds(keep, half), :] + core_in[g]
    size = half
    starts = [0] * GROUPS
    for phase, landing in enumerate((in_one, in_two, in_three)):
        size //= 4
        copies = []
        for g in range(GROUPS):
            axis = (g + phase) % 3
            copies.append([
                push(acc.at[g, pl.ds(pl.multiple_of(starts[g] + (coords[axis] + step) % 4 * size, size), size), :],
                     landing.at[g, step - 1], ring_sems, (phase, g, step - 1),
                     peer(axis, (coords[axis] + step) % 4))
                for step in range(1, 4)])
        for g in range(GROUPS):
            axis = (g + phase) % 3
            starts[g] = pl.multiple_of(starts[g] + coords[axis] * size, size)
            for copy in copies[g]:
                copy.wait()
            mine = pl.ds(starts[g], size)
            acc[g, mine, :] = (acc[g, mine, :] + landing[g, 0]) + (landing[g, 1] + landing[g, 2])
    bases = []
    for g in range(GROUPS):
        base = pl.multiple_of(g * per + core * half, half)
        bases.append(base)
        total[pl.ds(pl.multiple_of(base + starts[g], size), size), :] = acc[g, pl.ds(starts[g], size), :]
    for phase in (2, 1, 0):
        copies = []
        for g in range(GROUPS):
            axis = (g + phase) % 3
            span = total.at[pl.ds(pl.multiple_of(bases[g] + starts[g], size), size), :]
            copies.append([
                push(span, span, back_sems, (phase, g, step - 1), peer(axis, (coords[axis] + step) % 4))
                for step in range(1, 4)])
        for g in range(GROUPS):
            axis = (g + phase) % 3
            starts[g] = starts[g] - coords[axis] * size
            for copy in copies[g]:
                copy.wait()
        size *= 4
    copies = []
    for g in range(GROUPS):
        span = total.at[pl.ds(bases[g], half), :]
        copies.append(push(span, span, core_back, (g,), other))
    for copy in copies:
        copy.wait()
    final = pltpu.make_async_copy(total, out_ref, out_sem)
    final.start()
    final.wait()


def gram_sum(rows, collective_id):
    count, width = rows.shape
    nb = width // B
    half = SLOTS * B // GROUPS // 2
    return pl.pallas_call(
        functools.partial(gram_kernel, nb),
        out_shape=jax.ShapeDtypeStruct((SLOTS * B, B), F32),
        in_specs=[pl.BlockSpec(memory_space=pltpu.VMEM)],
        out_specs=pl.BlockSpec(memory_space=pl.ANY),
        scratch_shapes=[
            pltpu.VMEM((width, count), BF),
            pltpu.VMEM((SLOTS * B, B), F32),
            pltpu.VMEM((GROUPS, half, B), F32),
            pltpu.VMEM((GROUPS, half, B), F32),
            pltpu.VMEM((GROUPS, 3, half // 4, B), F32),
            pltpu.VMEM((GROUPS, 3, half // 16, B), F32),
            pltpu.VMEM((GROUPS, 3, half // 64, B), F32),
            pltpu.VMEM((SLOTS * B, B), F32),
            pltpu.SemaphoreType.DMA((2, GROUPS)),
            pltpu.SemaphoreType.DMA((2, 3, GROUPS, 3)),
            pltpu.SemaphoreType.DMA((2, 3, GROUPS, 3)),
            pltpu.SemaphoreType.DMA((2, GROUPS)),
            pltpu.SemaphoreType.DMA,
        ],
        compiler_params=pltpu.CompilerParams(
            collective_id=collective_id, has_side_effects=True, vmem_limit_bytes=48 * 1024 * 1024),
        cost_estimate=pl.CostEstimate(flops=2 * count * width * width, bytes_accessed=100_000_000, transcendentals=0),
    )(rows)

def factor_kernel(nb, rank, blocks_ref, *refs):
    low_ref = refs[0] if len(refs) == 6 else None
    inv_ref, work, linv, left, right = refs[-5:]
    npad = nb * B
    wid = npad + B
    work[:, npad:] = jnp.zeros((npad, B), F32)
    r0 = lax.broadcasted_iota(jnp.int32, (B, B), 0)
    r1 = lax.broadcasted_iota(jnp.int32, (B, B), 1)

    def unpack(q, carry):
        first, second = place(q, nb)
        block = blocks_ref[pl.ds(pl.multiple_of(q * B, B), B), :]
        a = pl.ds(pl.multiple_of(first * B, B), B)
        b = pl.ds(pl.multiple_of(second * B, B), B)
        work[b, a] = block.T
        work[a, b] = block
        return carry

    lax.fori_loop(0, nb * (nb + 1) // 2, unpack, 0)
    tail = slice(npad - B, npad)
    work[tail, tail] = jnp.where((r0 == r1) & (r0 >= rank - (npad - B)), 1.0, work[tail, tail])
    ri = lax.broadcasted_iota(jnp.int32, (npad, B), 0)

    def step(j, carry):
        at = pl.multiple_of(j * B, B)
        rows = pl.ds(at, B)
        diag = work[rows, rows]
        factor_inverse(diag, linv)
        inv = linv[...]
        h, m, l = split3(hdot(inv, work[rows, :], ((1,), (0,))))
        for q, part in enumerate((h, m, h, m, l, h)):
            right[q * B:(q + 1) * B, :] = part
        work[rows, :] = jnp.zeros((B, wid), F32)
        work[rows, rows] = jnp.where(r0 == r1, 1.0, 0.0).astype(F32)
        c = hdot(work[:, rows], inv, ((1,), (1,)))
        work[:, rows] = c
        if low_ref is not None:
            low_ref[:, rows] = jnp.where(ri >= at + B, c, 0.0).astype(low_ref.dtype)
            low_ref[rows, rows] = jnp.where(r0 >= r1, hdot(diag, inv, ((1,), (1,))), 0.0).astype(low_ref.dtype)
        h, m, l = split3(c)
        for q, part in enumerate((h, h, m, m, h, l)):
            left[:, q * B:(q + 1) * B] = part

        def chunk(q, carry):
            cols = pl.ds(pl.multiple_of((j + 1) * B + q * 2 * B, B), 2 * B)
            work[:, cols] = work[:, cols] - jnp.dot(left[...], right[:, cols], preferred_element_type=F32)
            return carry

        lax.fori_loop(0, (nb - j) // 2, chunk, 0)
        return carry

    lax.fori_loop(0, nb, step, 0)
    inv_ref[...] = work[:, :npad].astype(inv_ref.dtype)


def factor(blocks, width, rank, with_lower, kind):
    nb = width // B
    whole = jax.ShapeDtypeStruct((width, width), kind)
    results = (whole, whole) if with_lower else (whole,)
    return pl.pallas_call(
        functools.partial(factor_kernel, nb, rank),
        out_shape=results,
        in_specs=[pl.BlockSpec(memory_space=pltpu.VMEM)],
        out_specs=(pl.BlockSpec(memory_space=pltpu.VMEM),) * len(results),
        scratch_shapes=[
            pltpu.VMEM((width, width + B), F32),
            pltpu.VMEM((B, B), F32),
            pltpu.VMEM((width, 6 * B), BF),
            pltpu.VMEM((6 * B, width + B), BF),
        ],
        compiler_params=pltpu.CompilerParams(vmem_limit_bytes=56 * 1024 * 1024),
        cost_estimate=pl.CostEstimate(flops=20 * width**3, bytes_accessed=200_000_000, transcendentals=0),
    )(blocks)


def exact_dot(a, b, dims=((1,), (0,))):
    return hdot(a.astype(F32), b.astype(F32), dims)


def per_device(weight, test_matrix, fisher):
    row_count = lax.axis_size("row")
    col_count = lax.axis_size("col")
    col_index = lax.axis_index("col")
    block_rows = weight.shape[0]
    slice_rows = block_rows // col_count
    total_rows = block_rows * row_count
    total_cols = weight.shape[1] * col_count
    rank = test_matrix.shape[1]
    width = -(-rank // B) * B
    widen = ((0, 0), (0, width - rank))
    scales = jnp.sqrt(fisher)
    summed = lax.psum_scatter(
        jnp.dot(weight, test_matrix, preferred_element_type=F32).astype(BF),
        "col",
        scatter_dimension=0,
        tiled=True,
    ).astype(F32)
    own_scales = lax.dynamic_slice_in_dim(scales, col_index * slice_rows, slice_rows, 0)
    sketch = (own_scales[:, None] * summed).astype(BF)
    weighted_rows = (own_scales[:, None] * sketch.astype(F32)).astype(BF)
    weighted = lax.all_gather(weighted_rows, "col", axis=0, tiled=True)
    sketch = jnp.pad(sketch, widen)
    gram_one = gram_sum(sketch, 1)
    combos = lax.psum_scatter(
        lax.dot_general(
            weight, weighted, (((0,), (0,)), ((), ())), preferred_element_type=F32
        ).astype(BF),
        "row",
        scatter_dimension=0,
        tiled=True,
    ).astype(BF)
    all_combos = lax.all_gather(combos, "row", axis=0, tiled=True)
    gram_two = gram_sum(jnp.pad(combos, widen), 2)
    (upper_inv_one,) = factor(gram_one, width, rank, False, F32)
    basis = exact_dot(sketch, upper_inv_one)
    projected = exact_dot(basis, upper_inv_one, ((1,), (1,))).astype(BF)
    lower, upper_inv = factor(gram_two, width, rank, True, BF)
    right_factor = (
        math.sqrt(total_cols)
        * jnp.dot(all_combos, upper_inv[:rank, :rank], preferred_element_type=F32)
    ).astype(BF)
    product = jnp.dot(projected, lower[:, :rank], preferred_element_type=F32)
    left_factor = (math.sqrt(total_rows) * product / own_scales[:, None]).astype(BF)
    return (left_factor, right_factor)


def solution(mesh):
    return jax.shard_map(
        per_device,
        mesh=mesh,
        in_specs=(P("row", "col"), P("col", None), P("row")),
        out_specs=(P(("row", "col"), None), P("col", None)),
        check_vma=False,
    )
```

```python
import functools
import math

import jax
import jax.numpy as jnp
from jax import lax
from jax.experimental import pallas as pl
from jax.experimental.pallas import tpu as pltpu
from jax.sharding import PartitionSpec as P

F32 = jnp.float32
BF = jnp.bfloat16
B = 128

def factor_inverse(block, out_ref):
    groups = B // 8
    sub = lax.broadcasted_iota(jnp.int32, (8, B), 0)
    lane = lax.broadcasted_iota(jnp.int32, (8, B), 1)
    rows = [block[8 * t: 8 * t + 8, :] for t in range(groups)]
    inv = [jnp.where(lane == sub + 8 * t, 1.0, 0.0).astype(F32) for t in range(groups)]
    for p in range(groups):
        c0 = 8 * p
        cols = [[jnp.broadcast_to(rows[t][:, c0 + j: c0 + j + 1], (8, B)) for j in range(8)]
                for t in range(p, groups)]
        panel, wide = rows[p], inv[p]
        arow, wrow = [], []
        for j in range(8):
            own = cols[0][j]
            rinv = lax.rsqrt(jnp.broadcast_to(own[j:j + 1, :], (8, B)))
            for t in range(groups - p):
                cols[t][j] = cols[t][j] * rinv
            own = cols[0][j]
            for k in range(j + 1, 8):
                fac = jnp.broadcast_to(own[k:k + 1, :], (8, B))
                for t in range(groups - p):
                    cols[t][k] = cols[t][k] - cols[t][j] * fac
            ar = jnp.broadcast_to(panel[j:j + 1, :], (8, B)) * rinv
            wr = jnp.broadcast_to(wide[j:j + 1, :], (8, B)) * rinv
            arow.append(ar)
            wrow.append(wr)
            below = jnp.where(sub > j, own, 0.0)
            panel = panel - below * ar
            wide = jnp.where(sub == j, wr, wide - below * wr)
        inv[p] = wide
        for t in range(p + 1, groups):
            a, w = rows[t], inv[t]
            for j in range(8):
                a = a - cols[t - p][j] * arow[j]
                w = w - cols[t - p][j] * wrow[j]
            rows[t], inv[t] = a, w
    for t in range(groups):
        out_ref[8 * t: 8 * t + 8, :] = inv[t]

def split3(x):
    h = x.astype(BF)
    r = x - h.astype(F32)
    m = r.astype(BF)
    l = (r - m.astype(F32)).astype(BF)
    return h, m, l

def hdot(a, b, dims):
    return lax.dot_general(a, b, (dims, ((), ())), precision=lax.Precision.HIGHEST, preferred_element_type=F32)


SLOTS = 48
GROUPS = 3
MESH = pl.DeviceIdType.MESH


def place(q, nb):
    first = q % nb
    return first, (first + q // nb) % nb


def gram_kernel(nb, rows_ref, out_ref, turned, packed, core_in, acc, in_one, in_two, in_three, total,
                core_sems, ring_sems, back_sems, core_back, out_sem):
    row, col = lax.axis_index("row"), lax.axis_index("col")
    z, core, x, y = row // 2, row % 2, col // 4, col % 4
    coords = (x, y, z)

    def peer(axis, at):
        if axis == 0:
            return (row, at * 4 + y)
        if axis == 1:
            return (row, x * 4 + at)
        return (at * 2 + core, col)

    other = (z * 2 + 1 - core, col)
    barrier = pltpu.get_barrier_semaphore()
    pl.semaphore_signal(barrier, inc=1, device_id=other, device_id_type=MESH)
    for axis in range(3):
        for step in range(1, 4):
            pl.semaphore_signal(barrier, inc=1, device_id=peer(axis, (coords[axis] + step) % 4), device_id_type=MESH)

    turned[...] = rows_ref[...].astype(F32).T.astype(BF)

    def fill(q, carry):
        first, second = place(q, nb)
        block = jnp.dot(
            turned[pl.ds(pl.multiple_of(first * B, B), B), :],
            rows_ref[:, pl.ds(pl.multiple_of(second * B, B), B)],
            preferred_element_type=F32,
        )
        packed[pl.ds(pl.multiple_of(q * B, B), B), :] = block
        return carry

    used = nb * (nb + 1) // 2
    lax.fori_loop(0, used, fill, 0)
    packed[used * B:, :] = jnp.zeros(((SLOTS - used) * B, B), F32)
    pl.semaphore_wait(barrier, 10)

    per = SLOTS * B // GROUPS
    half = per // 2

    def push(src, dst, sems, index, device):
        copy = pltpu.make_async_remote_copy(
            src_ref=src, dst_ref=dst, send_sem=sems.at[(0,) + index], recv_sem=sems.at[(1,) + index],
            device_id=device, device_id_type=MESH)
        copy.start()
        return copy

    def core_push(g):
        away = pl.multiple_of(g * per + (1 - core) * half, half)
        return push(packed.at[pl.ds(away, half), :], core_in.at[g], core_sems, (g,), other)

    copies = [core_push(g) for g in range(GROUPS)]
    for g in range(GROUPS):
        copies[g].wait()
        keep = pl.multiple_of(g * per + core * half, half)
        acc[g] = packed[pl.ds(keep, half), :] + core_in[g]
    size = half
    starts = [0] * GROUPS
    for phase, landing in enumerate((in_one, in_two, in_three)):
        size //= 4
        copies = []
        for g in range(GROUPS):
            axis = (g + phase) % 3
            copies.append([
                push(acc.at[g, pl.ds(pl.multiple_of(starts[g] + (coords[axis] + step) % 4 * size, size), size), :],
                     landing.at[g, step - 1], ring_sems, (phase, g, step - 1),
                     peer(axis, (coords[axis] + step) % 4))
                for step in range(1, 4)])
        for g in range(GROUPS):
            axis = (g + phase) % 3
            starts[g] = pl.multiple_of(starts[g] + coords[axis] * size, size)
            for copy in copies[g]:
                copy.wait()
            mine = pl.ds(starts[g], size)
            acc[g, mine, :] = (acc[g, mine, :] + landing[g, 0]) + (landing[g, 1] + landing[g, 2])
    bases = []
    for g in range(GROUPS):
        base = pl.multiple_of(g * per + core * half, half)
        bases.append(base)
        total[pl.ds(pl.multiple_of(base + starts[g], size), size), :] = acc[g, pl.ds(starts[g], size), :]
    for phase in (2, 1, 0):
        copies = []
        for g in range(GROUPS):
            axis = (g + phase) % 3
            span = total.at[pl.ds(pl.multiple_of(bases[g] + starts[g], size), size), :]
            copies.append([
                push(span, span, back_sems, (phase, g, step - 1), peer(axis, (coords[axis] + step) % 4))
                for step in range(1, 4)])
        for g in range(GROUPS):
            axis = (g + phase) % 3
            starts[g] = starts[g] - coords[axis] * size
            for copy in copies[g]:
                copy.wait()
        size *= 4
    copies = []
    for g in range(GROUPS):
        span = total.at[pl.ds(bases[g], half), :]
        copies.append(push(span, span, core_back, (g,), other))
    for copy in copies:
        copy.wait()
    final = pltpu.make_async_copy(total, out_ref, out_sem)
    final.start()
    final.wait()


def gram_sum(rows, collective_id):
    count, width = rows.shape
    nb = width // B
    half = SLOTS * B // GROUPS // 2
    return pl.pallas_call(
        functools.partial(gram_kernel, nb),
        out_shape=jax.ShapeDtypeStruct((SLOTS * B, B), F32),
        in_specs=[pl.BlockSpec(memory_space=pltpu.VMEM)],
        out_specs=pl.BlockSpec(memory_space=pl.ANY),
        scratch_shapes=[
            pltpu.VMEM((width, count), BF),
            pltpu.VMEM((SLOTS * B, B), F32),
            pltpu.VMEM((GROUPS, half, B), F32),
            pltpu.VMEM((GROUPS, half, B), F32),
            pltpu.VMEM((GROUPS, 3, half // 4, B), F32),
            pltpu.VMEM((GROUPS, 3, half // 16, B), F32),
            pltpu.VMEM((GROUPS, 3, half // 64, B), F32),
            pltpu.VMEM((SLOTS * B, B), F32),
            pltpu.SemaphoreType.DMA((2, GROUPS)),
            pltpu.SemaphoreType.DMA((2, 3, GROUPS, 3)),
            pltpu.SemaphoreType.DMA((2, 3, GROUPS, 3)),
            pltpu.SemaphoreType.DMA((2, GROUPS)),
            pltpu.SemaphoreType.DMA,
        ],
        compiler_params=pltpu.CompilerParams(
            collective_id=collective_id, has_side_effects=True, vmem_limit_bytes=48 * 1024 * 1024),
        cost_estimate=pl.CostEstimate(flops=2 * count * width * width, bytes_accessed=100_000_000, transcendentals=0),
    )(rows)

def factor_kernel(nb, rank, blocks_ref, *refs):
    low_ref = refs[0] if len(refs) == 6 else None
    inv_ref, work, linv, left, right = refs[-5:]
    npad = nb * B
    wid = npad + B
    work[:, npad:] = jnp.zeros((npad, B), F32)
    r0 = lax.broadcasted_iota(jnp.int32, (B, B), 0)
    r1 = lax.broadcasted_iota(jnp.int32, (B, B), 1)

    def unpack(q, carry):
        first, second = place(q, nb)
        block = blocks_ref[pl.ds(pl.multiple_of(q * B, B), B), :]
        a = pl.ds(pl.multiple_of(first * B, B), B)
        b = pl.ds(pl.multiple_of(second * B, B), B)
        work[b, a] = block.T
        work[a, b] = block
        return carry

    lax.fori_loop(0, nb * (nb + 1) // 2, unpack, 0)
    tail = slice(npad - B, npad)
    work[tail, tail] = jnp.where((r0 == r1) & (r0 >= rank - (npad - B)), 1.0, work[tail, tail])
    ri = lax.broadcasted_iota(jnp.int32, (npad, B), 0)

    def step(j, carry):
        at = pl.multiple_of(j * B, B)
        rows = pl.ds(at, B)
        diag = work[rows, rows]
        factor_inverse(diag, linv)
        inv = linv[...]
        h, m, l = split3(hdot(inv, work[rows, :], ((1,), (0,))))
        for q, part in enumerate((h, m, h, m, l, h)):
            right[q * B:(q + 1) * B, :] = part
        work[rows, :] = jnp.zeros((B, wid), F32)
        work[rows, rows] = jnp.where(r0 == r1, 1.0, 0.0).astype(F32)
        c = hdot(work[:, rows], inv, ((1,), (1,)))
        work[:, rows] = c
        if low_ref is not None:
            low_ref[:, rows] = jnp.where(ri >= at + B, c, 0.0).astype(low_ref.dtype)
            low_ref[rows, rows] = jnp.where(r0 >= r1, hdot(diag, inv, ((1,), (1,))), 0.0).astype(low_ref.dtype)
        h, m, l = split3(c)
        for q, part in enumerate((h, h, m, m, h, l)):
            left[:, q * B:(q + 1) * B] = part

        def chunk(q, carry):
            cols = pl.ds(pl.multiple_of((j + 1) * B + q * 2 * B, B), 2 * B)
            work[:, cols] = work[:, cols] - jnp.dot(left[...], right[:, cols], preferred_element_type=F32)
            return carry

        lax.fori_loop(0, (nb - j) // 2, chunk, 0)
        return carry

    lax.fori_loop(0, nb, step, 0)
    full = work[:, :npad]
    if low_ref is not None:
        inv_ref[...] = full.astype(BF)
    else:
        inv_ref[0] = full.astype(BF)
        inv_ref[1] = (full - full.astype(BF).astype(F32)).astype(BF)


def factor(blocks, width, rank, with_lower):
    nb = width // B
    whole = jax.ShapeDtypeStruct((width, width), BF)
    results = (whole, whole) if with_lower else (jax.ShapeDtypeStruct((2, width, width), BF),)
    return pl.pallas_call(
        functools.partial(factor_kernel, nb, rank),
        out_shape=results,
        in_specs=[pl.BlockSpec(memory_space=pltpu.VMEM)],
        out_specs=(pl.BlockSpec(memory_space=pltpu.VMEM),) * len(results),
        scratch_shapes=[
            pltpu.VMEM((width, width + B), F32),
            pltpu.VMEM((B, B), F32),
            pltpu.VMEM((width, 6 * B), BF),
            pltpu.VMEM((6 * B, width + B), BF),
        ],
        compiler_params=pltpu.CompilerParams(vmem_limit_bytes=56 * 1024 * 1024),
        cost_estimate=pl.CostEstimate(flops=20 * width**3, bytes_accessed=200_000_000, transcendentals=0),
    )(blocks)


def split_dot(a, parts, dims):
    return sum(
        lax.dot_general(a, parts[i], (dims, ((), ())), preferred_element_type=F32) for i in range(2)
    )


def per_device(weight, test_matrix, fisher):
    row_count = lax.axis_size("row")
    col_count = lax.axis_size("col")
    col_index = lax.axis_index("col")
    block_rows = weight.shape[0]
    slice_rows = block_rows // col_count
    total_rows = block_rows * row_count
    total_cols = weight.shape[1] * col_count
    rank = test_matrix.shape[1]
    width = -(-rank // B) * B
    widen = ((0, 0), (0, width - rank))
    scales = jnp.sqrt(fisher)
    summed = lax.psum_scatter(
        jnp.dot(weight, test_matrix, preferred_element_type=F32).astype(BF),
        "col",
        scatter_dimension=0,
        tiled=True,
    ).astype(F32)
    own_scales = lax.dynamic_slice_in_dim(scales, col_index * slice_rows, slice_rows, 0)
    sketch = (own_scales[:, None] * summed).astype(BF)
    weighted_rows = (own_scales[:, None] * sketch.astype(F32)).astype(BF)
    weighted = lax.all_gather(weighted_rows, "col", axis=0, tiled=True)
    sketch = jnp.pad(sketch, widen)
    gram_one = gram_sum(sketch, 1)
    weighted, gram_one = lax.optimization_barrier((weighted, gram_one))
    combos = lax.psum_scatter(
        lax.dot_general(
            weight, weighted, (((0,), (0,)), ((), ())), preferred_element_type=F32
        ).astype(BF),
        "row",
        scatter_dimension=0,
        tiled=True,
    ).astype(BF)
    all_combos = lax.all_gather(combos, "row", axis=0, tiled=True)
    gram_two = gram_sum(jnp.pad(combos, widen), 2)
    (upper_inv_one,) = factor(gram_one, width, rank, False)
    basis = split_dot(sketch, upper_inv_one, ((1,), (0,))).astype(BF)
    projected = split_dot(basis, upper_inv_one, ((1,), (1,))).astype(BF)
    lower, upper_inv = factor(gram_two, width, rank, True)
    right_factor = (
        math.sqrt(total_cols)
        * jnp.dot(all_combos, upper_inv[:rank, :rank], preferred_element_type=F32)
    ).astype(BF)
    product = jnp.dot(projected, lower[:, :rank], preferred_element_type=F32)
    left_factor = (math.sqrt(total_rows) * product / own_scales[:, None]).astype(BF)
    return (left_factor, right_factor)


def solution(mesh):
    return jax.shard_map(
        per_device,
        mesh=mesh,
        in_specs=(P("row", "col"), P("col", None), P("row")),
        out_specs=(P(("row", "col"), None), P("col", None)),
        check_vma=False,
    )
```

```python
import functools
import math

import jax
import jax.numpy as jnp
from jax import lax
from jax.experimental import pallas as pl
from jax.experimental.pallas import tpu as pltpu
from jax.sharding import PartitionSpec as P

F32 = jnp.float32
BF = jnp.bfloat16
B = 128

def factor_inverse(block, out_ref, others=()):
    groups = B // 8
    sub = lax.broadcasted_iota(jnp.int32, (8, B), 0)
    lane = lax.broadcasted_iota(jnp.int32, (8, B), 1)
    rows = [block[8 * t: 8 * t + 8, :] for t in range(groups)]
    inv = [jnp.where(lane == sub + 8 * t, 1.0, 0.0).astype(F32) for t in range(groups)]
    given = 0
    for p in range(groups):
        while given < len(others) and given * groups <= p * len(others):
            others[given]()
            given += 1
        c0 = 8 * p
        cols = [[jnp.broadcast_to(rows[t][:, c0 + j: c0 + j + 1], (8, B)) for j in range(8)]
                for t in range(p, groups)]
        panel, wide = rows[p], inv[p]
        arow, wrow = [], []
        for j in range(8):
            own = cols[0][j]
            rinv = lax.rsqrt(jnp.broadcast_to(own[j:j + 1, :], (8, B)))
            for t in range(groups - p):
                cols[t][j] = cols[t][j] * rinv
            own = cols[0][j]
            for k in range(j + 1, 8):
                fac = jnp.broadcast_to(own[k:k + 1, :], (8, B))
                for t in range(groups - p):
                    cols[t][k] = cols[t][k] - cols[t][j] * fac
            ar = jnp.broadcast_to(panel[j:j + 1, :], (8, B)) * rinv
            wr = jnp.broadcast_to(wide[j:j + 1, :], (8, B)) * rinv
            arow.append(ar)
            wrow.append(wr)
            below = jnp.where(sub > j, own, 0.0)
            panel = panel - below * ar
            wide = jnp.where(sub == j, wr, wide - below * wr)
        inv[p] = wide
        for t in range(p + 1, groups):
            a, w = rows[t], inv[t]
            for j in range(8):
                a = a - cols[t - p][j] * arow[j]
                w = w - cols[t - p][j] * wrow[j]
            rows[t], inv[t] = a, w
    for item in others[given:]:
        item()
    for t in range(groups):
        out_ref[8 * t: 8 * t + 8, :] = inv[t]

def split3(x):
    h = x.astype(BF)
    r = x - h.astype(F32)
    m = r.astype(BF)
    l = (r - m.astype(F32)).astype(BF)
    return h, m, l

def hdot(a, b, dims):
    return lax.dot_general(a, b, (dims, ((), ())), precision=lax.Precision.HIGHEST, preferred_element_type=F32)


SLOTS = 48
PARTS = 1
GROUPS = 3
MESH = pl.DeviceIdType.MESH


def place(q, nb):
    first = q % nb
    return first, (first + q // nb) % nb


def gram_kernel(nb, rows_ref, out_ref, turned, packed, core_in, acc, in_one, in_two, in_three, total,
                core_sems, ring_sems, back_sems, core_back, out_sem):
    row, col = lax.axis_index("row"), lax.axis_index("col")
    z, core, x, y = row // 2, row % 2, col // 4, col % 4
    coords = (x, y, z)

    def peer(axis, at):
        if axis == 0:
            return (row, at * 4 + y)
        if axis == 1:
            return (row, x * 4 + at)
        return (at * 2 + core, col)

    other = (z * 2 + 1 - core, col)
    barrier = pltpu.get_barrier_semaphore()
    pl.semaphore_signal(barrier, inc=1, device_id=other, device_id_type=MESH)
    for axis in range(3):
        for step in range(1, 4):
            pl.semaphore_signal(barrier, inc=1, device_id=peer(axis, (coords[axis] + step) % 4), device_id_type=MESH)

    turned[...] = rows_ref[...].astype(F32).T.astype(BF)

    def fill(q, carry):
        first, second = place(q, nb)
        block = jnp.dot(
            turned[pl.ds(pl.multiple_of(first * B, B), B), :],
            rows_ref[:, pl.ds(pl.multiple_of(second * B, B), B)],
            preferred_element_type=F32,
        )
        packed[pl.ds(pl.multiple_of(q * B, B), B), :] = block
        return carry

    used = nb * (nb + 1) // 2
    lax.fori_loop(0, used, fill, 0)
    packed[used * B:, :] = jnp.zeros(((SLOTS - used) * B, B), F32)
    pl.semaphore_wait(barrier, 10)

    per = SLOTS * B // GROUPS
    half = per // 2

    def push(src, dst, sems, index, device):
        copy = pltpu.make_async_remote_copy(
            src_ref=src, dst_ref=dst, send_sem=sems.at[(0,) + index], recv_sem=sems.at[(1,) + index],
            device_id=device, device_id_type=MESH)
        copy.start()
        return copy

    def core_push(g):
        away = pl.multiple_of(g * per + (1 - core) * half, half)
        return push(packed.at[pl.ds(away, half), :], core_in.at[g], core_sems, (g,), other)

    copies = [core_push(g) for g in range(GROUPS)]
    for g in range(GROUPS):
        copies[g].wait()
        keep = pl.multiple_of(g * per + core * half, half)
        acc[g] = packed[pl.ds(keep, half), :] + core_in[g]
    size = half
    starts = [0] * GROUPS
    for phase, landing in enumerate((in_one, in_two, in_three)):
        size //= 4
        copies = []
        for g in range(GROUPS):
            axis = (g + phase) % 3
            copies.append([
                push(acc.at[g, pl.ds(pl.multiple_of(starts[g] + (coords[axis] + step) % 4 * size, size), size), :],
                     landing.at[g, step - 1], ring_sems, (phase, g, step - 1),
                     peer(axis, (coords[axis] + step) % 4))
                for step in range(1, 4)])
        for g in range(GROUPS):
            axis = (g + phase) % 3
            starts[g] = pl.multiple_of(starts[g] + coords[axis] * size, size)
            for copy in copies[g]:
                copy.wait()
            mine = pl.ds(starts[g], size)
            acc[g, mine, :] = (acc[g, mine, :] + landing[g, 0]) + (landing[g, 1] + landing[g, 2])
    bases = []
    for g in range(GROUPS):
        base = pl.multiple_of(g * per + core * half, half)
        bases.append(base)
        total[pl.ds(pl.multiple_of(base + starts[g], size), size), :] = acc[g, pl.ds(starts[g], size), :]
    for phase in (2, 1, 0):
        copies = []
        for g in range(GROUPS):
            axis = (g + phase) % 3
            span = total.at[pl.ds(pl.multiple_of(bases[g] + starts[g], size), size), :]
            copies.append([
                push(span, span, back_sems, (phase, g, step - 1), peer(axis, (coords[axis] + step) % 4))
                for step in range(1, 4)])
        for g in range(GROUPS):
            axis = (g + phase) % 3
            starts[g] = starts[g] - coords[axis] * size
            for copy in copies[g]:
                copy.wait()
        size *= 4
    copies = []
    for g in range(GROUPS):
        span = total.at[pl.ds(bases[g], half), :]
        copies.append(push(span, span, core_back, (g,), other))
    for copy in copies:
        copy.wait()
    final = pltpu.make_async_copy(total, out_ref, out_sem)
    final.start()
    final.wait()


def gram_sum(rows, collective_id):
    count, width = rows.shape
    nb = width // B
    half = SLOTS * B // GROUPS // 2
    return pl.pallas_call(
        functools.partial(gram_kernel, nb),
        out_shape=jax.ShapeDtypeStruct((SLOTS * B, B), F32),
        in_specs=[pl.BlockSpec(memory_space=pltpu.VMEM)],
        out_specs=pl.BlockSpec(memory_space=pl.ANY),
        scratch_shapes=[
            pltpu.VMEM((width, count), BF),
            pltpu.VMEM((SLOTS * B, B), F32),
            pltpu.VMEM((GROUPS, half, B), F32),
            pltpu.VMEM((GROUPS, half, B), F32),
            pltpu.VMEM((GROUPS, 3, half // 4, B), F32),
            pltpu.VMEM((GROUPS, 3, half // 16, B), F32),
            pltpu.VMEM((GROUPS, 3, half // 64, B), F32),
            pltpu.VMEM((SLOTS * B, B), F32),
            pltpu.SemaphoreType.DMA((2, GROUPS)),
            pltpu.SemaphoreType.DMA((2, 3, GROUPS, 3)),
            pltpu.SemaphoreType.DMA((2, 3, GROUPS, 3)),
            pltpu.SemaphoreType.DMA((2, GROUPS)),
            pltpu.SemaphoreType.DMA,
        ],
        compiler_params=pltpu.CompilerParams(
            collective_id=collective_id, has_side_effects=True, vmem_limit_bytes=48 * 1024 * 1024),
        cost_estimate=pl.CostEstimate(flops=2 * count * width * width, bytes_accessed=100_000_000, transcendentals=0),
    )(rows)

def sketch_kernel(rank, w_hbm, turned_hbm, scale_ref, sketch_ref, weighted_ref, w, turned, part, relay, land, last,
                  w_sems, turned_sem, relay_sems, land_sems, last_sems):
    row, col = lax.axis_index("row"), lax.axis_index("col")
    coords = (col // 4, col % 4)
    lines = w.shape[3]
    width = turned.shape[0]

    def peer(axis, at):
        return (row, at * 4 + coords[1]) if axis == 0 else (row, coords[0] * 4 + at)

    def ahead(axis, step):
        return lax.rem(coords[axis] + step, 4)

    barrier = pltpu.get_barrier_semaphore()
    for axis in range(2):
        for step in range(1, 4):
            pl.semaphore_signal(barrier, inc=1, device_id=peer(axis, ahead(axis, step)), device_id_type=MESH)

    fetch_turned = pltpu.make_async_copy(turned_hbm, turned.at[pl.ds(0, rank), :], turned_sem)
    fetch_turned.start()
    fetches = {}
    order = [(side, step) for step in (2, 1, 3, 0) for side in range(2)]
    for side, step in order:
        at = ahead(side, step)
        fetches[side, step] = []
        for b in range(4):
            chunk = at * 4 + b if side == 0 else b * 4 + at
            copy = pltpu.make_async_copy(
                w_hbm.at[pl.ds(pl.multiple_of(chunk * 2 * lines + side * lines, 16), lines), :],
                w.at[side, at, b], w_sems.at[side, step, b])
            copy.start()
            fetches[side, step].append(copy)
    turned[rank:, :] = jnp.zeros((width - rank, turned.shape[1]), BF)
    fetch_turned.wait()

    def product(side, step):
        at = ahead(side, step)
        for copy in fetches[side, step]:
            copy.wait()

        def some(q, carry):
            cols = pl.ds(pl.multiple_of(q * 3 * B, B), 3 * B)
            result = lax.dot_general(
                w[side, at].reshape(4 * lines, w.shape[4]), turned[cols, :], (((1,), (1,)), ((), ())),
                preferred_element_type=F32)
            part[side, at, :, :, cols] = result.astype(BF).reshape(4, lines, 3 * B)
            return carry

        lax.fori_loop(0, width // (3 * B), some, 0)

    copies = []

    def push(src, dst, sems, index, device):
        copy = pltpu.make_async_remote_copy(
            src_ref=src, dst_ref=dst, send_sem=sems.at[(0,) + index], recv_sem=sems.at[(1,) + index],
            device_id=device, device_id_type=MESH)
        copy.start()
        copies.append(copy)
        return copy

    relays, lands = {}, {}
    for side, step in order:
        product(side, step)
        at = ahead(side, step)
        if (side, step) == (0, 2):
            pl.semaphore_wait(barrier, 6)
        if step == 2:
            for way, near in ((0, 1), (1, 3)):
                relays[side, way] = push(
                    part.at[side, at, pl.ds(2 * way, 2)], relay.at[side, way], relay_sems, (side, way),
                    peer(side, ahead(side, near)))
        elif step != 0:
            way = 0 if step == 1 else 1
            half = 1 - way
            lands[side, way, half] = push(
                part.at[side, at, pl.ds(2 * half, 2)], land.at[side, way, pl.ds(2 * half, 2)], land_sems,
                (side, way, half), peer(side, at))
    for side in range(2):
        for way, step in ((0, 1), (1, 3)):
            at = ahead(side, step)
            relays[side, way].wait_recv()
            for b in range(2):
                mine = part[side, at, 2 * way + b].astype(F32)
                part[side, at, 2 * way + b] = (mine + relay[side, way, b].astype(F32)).astype(BF)
            lands[side, way, way] = push(
                part.at[side, at, pl.ds(2 * way, 2)], land.at[side, way, pl.ds(2 * way, 2)], land_sems,
                (side, way, way), peer(side, at))
    lasts = {}
    for side in range(2):
        for way in range(2):
            for half in (1 - way, way):
                lands[side, way, half].wait_recv()
        for step in (2, 1, 3):
            at = ahead(1 - side, step)
            total = part[side, coords[side], at].astype(F32) + (
                land[side, 0, at].astype(F32) + land[side, 1, at].astype(F32))
            part[side, coords[side], at] = total.astype(BF)
            lasts[side, step] = push(
                part.at[side, coords[side], at], last.at[side, step - 1], last_sems, (side, step - 1),
                peer(1 - side, at))
    for side in range(2):
        at = coords[1 - side]
        total = part[side, coords[side], at].astype(F32) + (
            land[side, 0, at].astype(F32) + land[side, 1, at].astype(F32))
        for step in (1, 3, 2):
            lasts[side, step].wait_recv()
        total = total + ((last[side, 0].astype(F32) + last[side, 1].astype(F32)) + last[side, 2].astype(F32))
        mine = slice(side * lines, side * lines + lines)
        scale = scale_ref[mine, :]
        sketch = (scale * total).astype(BF)
        sketch_ref[mine, :] = sketch
        weighted_ref[mine, :] = (scale * sketch.astype(F32)).astype(BF)
    for copy in copies:
        copy.wait_send()


def sketch_rows(weight, test_matrix, own_scales, width, collective_id):
    block_rows, depth = weight.shape
    rank = test_matrix.shape[1]
    count = own_scales.shape[0]
    lines = count // 2
    result = jax.ShapeDtypeStruct((count, width), BF)
    vmem = pl.BlockSpec(memory_space=pltpu.VMEM)
    return pl.pallas_call(
        functools.partial(sketch_kernel, rank),
        out_shape=(result, result),
        in_specs=[pl.BlockSpec(memory_space=pl.ANY), pl.BlockSpec(memory_space=pl.ANY), vmem],
        out_specs=(vmem, vmem),
        scratch_shapes=[
            pltpu.VMEM((2, 4, 4, lines, depth), BF),
            pltpu.VMEM((width, depth), BF),
            pltpu.VMEM((2, 4, 4, lines, width), BF),
            pltpu.VMEM((2, 2, 2, lines, width), BF),
            pltpu.VMEM((2, 2, 4, lines, width), BF),
            pltpu.VMEM((2, 3, lines, width), BF),
            pltpu.SemaphoreType.DMA((2, 4, 4)),
            pltpu.SemaphoreType.DMA,
            pltpu.SemaphoreType.DMA((2, 2, 2)),
            pltpu.SemaphoreType.DMA((2, 2, 2, 2)),
            pltpu.SemaphoreType.DMA((2, 2, 3)),
        ],
        compiler_params=pltpu.CompilerParams(
            collective_id=collective_id, has_side_effects=True, vmem_limit_bytes=60 * 1024 * 1024),
        cost_estimate=pl.CostEstimate(flops=2 * block_rows * depth * width, bytes_accessed=100_000_000, transcendentals=0),
    )(weight, test_matrix.T, own_scales[:, None])


def factor_kernel(nb, rank, blocks_ref, *refs):
    low_ref = refs[0] if len(refs) == 6 else None
    inv_ref, work, linv, left, right = refs[-5:]
    npad = nb * B
    wid = npad + 2 * B
    work[:, npad:] = jnp.zeros((npad, wid - npad), F32)
    right[:, npad:] = jnp.zeros((6 * B, wid - npad), BF)
    r0 = lax.broadcasted_iota(jnp.int32, (B, B), 0)
    r1 = lax.broadcasted_iota(jnp.int32, (B, B), 1)
    ri = lax.broadcasted_iota(jnp.int32, (npad, B), 0)

    def unpack(q):
        first, second = place(q, nb)
        block = blocks_ref[q * B:(q + 1) * B, :]
        if first == second == nb - 1:
            block = jnp.where((r0 == r1) & (r0 >= rank - (npad - B)), 1.0, block)
        a, b = slice(first * B, first * B + B), slice(second * B, second * B + B)
        work[a, b] = block
        if first != second:
            work[b, a] = block.T

    factor_inverse(blocks_ref[0:B, :], linv, [functools.partial(unpack, q) for q in range(nb * (nb + 1) // 2)])

    def spread(j, rows, inv, diag):
        c = hdot(work[:, rows], inv, ((1,), (1,)))
        work[:, rows] = c
        if low_ref is not None:
            low_ref[:, rows] = jnp.where(ri >= j * B + B, c, 0.0).astype(low_ref.dtype)
            low_ref[rows, rows] = jnp.where(r0 >= r1, hdot(diag, inv, ((1,), (1,))), 0.0).astype(low_ref.dtype)
        return c

    def step(pieces, j, carry):
        rows = pl.ds(pl.multiple_of(j * B, B), B)
        after = pl.ds(pl.multiple_of(j * B + B, B), B)
        inv = linv[...]
        diag = work[rows, rows]
        next_u = hdot(inv, work[rows, after], ((1,), (0,)))
        next_c = hdot(work[after, rows], inv, ((1,), (1,)))
        next_diag = work[after, after] - hdot(next_c, next_u, ((1,), (0,)))

        def across():
            h, m, l = split3(hdot(inv, work[rows, :npad], ((1,), (0,))))
            for q, part in enumerate((h, m, h, m, l, h)):
                right[q * B:(q + 1) * B, :npad] = part
            work[rows, :] = jnp.zeros((B, wid), F32)
            work[rows, rows] = jnp.where(r0 == r1, 1.0, 0.0).astype(F32)

        def down():
            h, m, l = split3(spread(j, rows, inv, diag))
            for q, part in enumerate((h, h, m, m, h, l)):
                left[:, q * B:(q + 1) * B] = part

        def update(q, top):
            cols = pl.ds(pl.multiple_of(jnp.minimum((j + 1) * B + q * 2 * B, npad), B), 2 * B)
            lines = slice(top, top + HALF)
            work[lines, cols] = work[lines, cols] - jnp.dot(
                left[lines, :], right[:, cols], preferred_element_type=F32)

        HALF = npad // PARTS
        work_items = [across, down] + [
            functools.partial(update, q, part * HALF) for q in range(pieces) for part in range(PARTS)]
        factor_inverse(next_diag, linv, work_items)
        return carry

    early = nb // 2
    lax.fori_loop(0, early, functools.partial(step, nb // 2), 0)
    lax.fori_loop(early, nb - 1, functools.partial(step, (nb - early) // 2), 0)
    rows = slice(npad - B, npad)
    diag = work[rows, rows]
    work[rows, :] = jnp.zeros((B, wid), F32)
    work[rows, rows] = jnp.where(r0 == r1, 1.0, 0.0).astype(F32)
    spread(nb - 1, rows, linv[...], diag)
    full = work[:, :npad]
    if low_ref is not None:
        inv_ref[...] = full.astype(BF)
    else:
        inv_ref[0] = full.astype(BF)
        inv_ref[1] = (full - full.astype(BF).astype(F32)).astype(BF)


def factor(blocks, width, rank, with_lower):
    nb = width // B
    whole = jax.ShapeDtypeStruct((width, width), BF)
    results = (whole, whole) if with_lower else (jax.ShapeDtypeStruct((2, width, width), BF),)
    return pl.pallas_call(
        functools.partial(factor_kernel, nb, rank),
        out_shape=results,
        in_specs=[pl.BlockSpec(memory_space=pltpu.VMEM)],
        out_specs=(pl.BlockSpec(memory_space=pltpu.VMEM),) * len(results),
        scratch_shapes=[
            pltpu.VMEM((width, width + 2 * B), F32),
            pltpu.VMEM((B, B), F32),
            pltpu.VMEM((width, 6 * B), BF),
            pltpu.VMEM((6 * B, width + 2 * B), BF),
        ],
        compiler_params=pltpu.CompilerParams(vmem_limit_bytes=56 * 1024 * 1024),
        cost_estimate=pl.CostEstimate(flops=20 * width**3, bytes_accessed=200_000_000, transcendentals=0),
    )(blocks)


def split_dot(a, parts, dims):
    return sum(
        lax.dot_general(a, parts[i], (dims, ((), ())), preferred_element_type=F32) for i in range(2)
    )


def per_device(weight, test_matrix, fisher):
    row_count = lax.axis_size("row")
    col_count = lax.axis_size("col")
    col_index = lax.axis_index("col")
    block_rows = weight.shape[0]
    slice_rows = block_rows // col_count
    total_rows = block_rows * row_count
    total_cols = weight.shape[1] * col_count
    rank = test_matrix.shape[1]
    width = -(-rank // B) * B
    scales = jnp.sqrt(fisher)
    own_scales = lax.dynamic_slice_in_dim(scales, col_index * slice_rows, slice_rows, 0)
    sketch, weighted_rows = sketch_rows(weight, test_matrix, own_scales, width, 3)
    weighted = lax.all_gather(weighted_rows, "col", axis=0, tiled=True)
    gram_one = gram_sum(sketch, 1)
    weighted, gram_one = lax.optimization_barrier((weighted, gram_one))
    combos = lax.psum_scatter(
        lax.dot_general(
            weight, weighted, (((0,), (0,)), ((), ())), preferred_element_type=F32
        ).astype(BF),
        "row",
        scatter_dimension=0,
        tiled=True,
    ).astype(BF)
    all_combos = lax.all_gather(combos, "row", axis=0, tiled=True)
    gram_two = gram_sum(combos, 2)
    (upper_inv_one,) = factor(gram_one, width, rank, False)
    basis = split_dot(sketch, upper_inv_one, ((1,), (0,))).astype(BF)
    projected = split_dot(basis, upper_inv_one, ((1,), (1,))).astype(BF)
    lower, upper_inv = factor(gram_two, width, rank, True)
    right_factor = (
        math.sqrt(total_cols)
        * jnp.dot(all_combos, upper_inv[:, :rank], preferred_element_type=F32)
    ).astype(BF)
    product = jnp.dot(projected, lower[:, :rank], preferred_element_type=F32)
    left_factor = (math.sqrt(total_rows) * product / own_scales[:, None]).astype(BF)
    return (left_factor, right_factor)


def solution(mesh):
    return jax.shard_map(
        per_device,
        mesh=mesh,
        in_specs=(P("row", "col"), P("col", None), P("row")),
        out_specs=(P(("row", "col"), None), P("col", None)),
        check_vma=False,
    )
```

```python
import functools
import math

import jax
import jax.numpy as jnp
from jax import lax
from jax.experimental import pallas as pl
from jax.experimental.pallas import tpu as pltpu
from jax.sharding import PartitionSpec as P

F32 = jnp.float32
BF = jnp.bfloat16
B = 128

def factor_inverse(block, out_ref, others=()):
    groups = B // 8
    sub = lax.broadcasted_iota(jnp.int32, (8, B), 0)
    lane = lax.broadcasted_iota(jnp.int32, (8, B), 1)
    rows = [block[8 * t: 8 * t + 8, :] for t in range(groups)]
    inv = [jnp.where(lane == sub + 8 * t, 1.0, 0.0).astype(F32) for t in range(groups)]
    given = 0
    for p in range(groups):
        while given < len(others) and given * groups <= p * len(others):
            others[given]()
            given += 1
        c0 = 8 * p
        cols = [[jnp.broadcast_to(rows[t][:, c0 + j: c0 + j + 1], (8, B)) for j in range(8)]
                for t in range(p, groups)]
        panel, wide = rows[p], inv[p]
        arow, wrow = [], []
        for j in range(8):
            own = cols[0][j]
            rinv = lax.rsqrt(jnp.broadcast_to(own[j:j + 1, :], (8, B)))
            for t in range(groups - p):
                cols[t][j] = cols[t][j] * rinv
            own = cols[0][j]
            for k in range(j + 1, 8):
                fac = jnp.broadcast_to(own[k:k + 1, :], (8, B))
                for t in range(groups - p):
                    cols[t][k] = cols[t][k] - cols[t][j] * fac
            ar = jnp.broadcast_to(panel[j:j + 1, :], (8, B)) * rinv
            wr = jnp.broadcast_to(wide[j:j + 1, :], (8, B)) * rinv
            arow.append(ar)
            wrow.append(wr)
            below = jnp.where(sub > j, own, 0.0)
            panel = panel - below * ar
            wide = jnp.where(sub == j, wr, wide - below * wr)
        inv[p] = wide
        for t in range(p + 1, groups):
            a, w = rows[t], inv[t]
            for j in range(8):
                a = a - cols[t - p][j] * arow[j]
                w = w - cols[t - p][j] * wrow[j]
            rows[t], inv[t] = a, w
    for item in others[given:]:
        item()
    for t in range(groups):
        out_ref[8 * t: 8 * t + 8, :] = inv[t]

def split3(x):
    h = x.astype(BF)
    r = x - h.astype(F32)
    m = r.astype(BF)
    l = (r - m.astype(F32)).astype(BF)
    return h, m, l

def hdot(a, b, dims):
    return lax.dot_general(a, b, (dims, ((), ())), precision=lax.Precision.HIGHEST, preferred_element_type=F32)


SLOTS = 48
PARTS = 1
GROUPS = 3
MESH = pl.DeviceIdType.MESH


def place(q, nb):
    first = q % nb
    return first, (first + q // nb) % nb


def gram_kernel(nb, rows_ref, out_ref, turned, packed, core_in, acc, in_one, in_two, in_three, total,
                core_sems, ring_sems, back_sems, core_back, out_sem):
    row, col = lax.axis_index("row"), lax.axis_index("col")
    z, core, x, y = row // 2, row % 2, col // 4, col % 4
    coords = (x, y, z)

    def peer(axis, at):
        if axis == 0:
            return (row, at * 4 + y)
        if axis == 1:
            return (row, x * 4 + at)
        return (at * 2 + core, col)

    other = (z * 2 + 1 - core, col)
    barrier = pltpu.get_barrier_semaphore()
    pl.semaphore_signal(barrier, inc=1, device_id=other, device_id_type=MESH)
    for axis in range(3):
        for step in range(1, 4):
            pl.semaphore_signal(barrier, inc=1, device_id=peer(axis, (coords[axis] + step) % 4), device_id_type=MESH)

    turned[...] = rows_ref[...].astype(F32).T.astype(BF)

    def fill(q, carry):
        first, second = place(q, nb)
        block = jnp.dot(
            turned[pl.ds(pl.multiple_of(first * B, B), B), :],
            rows_ref[:, pl.ds(pl.multiple_of(second * B, B), B)],
            preferred_element_type=F32,
        )
        packed[pl.ds(pl.multiple_of(q * B, B), B), :] = block
        return carry

    used = nb * (nb + 1) // 2
    lax.fori_loop(0, used, fill, 0)
    packed[used * B:, :] = jnp.zeros(((SLOTS - used) * B, B), F32)
    pl.semaphore_wait(barrier, 10)

    per = SLOTS * B // GROUPS
    half = per // 2

    def push(src, dst, sems, index, device):
        copy = pltpu.make_async_remote_copy(
            src_ref=src, dst_ref=dst, send_sem=sems.at[(0,) + index], recv_sem=sems.at[(1,) + index],
            device_id=device, device_id_type=MESH)
        copy.start()
        return copy

    def core_push(g):
        away = pl.multiple_of(g * per + (1 - core) * half, half)
        return push(packed.at[pl.ds(away, half), :], core_in.at[g], core_sems, (g,), other)

    copies = [core_push(g) for g in range(GROUPS)]
    for g in range(GROUPS):
        copies[g].wait()
        keep = pl.multiple_of(g * per + core * half, half)
        acc[g] = packed[pl.ds(keep, half), :] + core_in[g]
    size = half
    starts = [0] * GROUPS
    for phase, landing in enumerate((in_one, in_two, in_three)):
        size //= 4
        copies = []
        for g in range(GROUPS):
            axis = (g + phase) % 3
            copies.append([
                push(acc.at[g, pl.ds(pl.multiple_of(starts[g] + (coords[axis] + step) % 4 * size, size), size), :],
                     landing.at[g, step - 1], ring_sems, (phase, g, step - 1),
                     peer(axis, (coords[axis] + step) % 4))
                for step in range(1, 4)])
        for g in range(GROUPS):
            axis = (g + phase) % 3
            starts[g] = pl.multiple_of(starts[g] + coords[axis] * size, size)
            for copy in copies[g]:
                copy.wait()
            mine = pl.ds(starts[g], size)
            acc[g, mine, :] = (acc[g, mine, :] + landing[g, 0]) + (landing[g, 1] + landing[g, 2])
    bases = []
    for g in range(GROUPS):
        base = pl.multiple_of(g * per + core * half, half)
        bases.append(base)
        total[pl.ds(pl.multiple_of(base + starts[g], size), size), :] = acc[g, pl.ds(starts[g], size), :]
    for phase in (2, 1, 0):
        copies = []
        for g in range(GROUPS):
            axis = (g + phase) % 3
            span = total.at[pl.ds(pl.multiple_of(bases[g] + starts[g], size), size), :]
            copies.append([
                push(span, span, back_sems, (phase, g, step - 1), peer(axis, (coords[axis] + step) % 4))
                for step in range(1, 4)])
        for g in range(GROUPS):
            axis = (g + phase) % 3
            starts[g] = starts[g] - coords[axis] * size
            for copy in copies[g]:
                copy.wait()
        size *= 4
    copies = []
    for g in range(GROUPS):
        span = total.at[pl.ds(bases[g], half), :]
        copies.append(push(span, span, core_back, (g,), other))
    for copy in copies:
        copy.wait()
    final = pltpu.make_async_copy(total, out_ref, out_sem)
    final.start()
    final.wait()


def gram_sum(rows, collective_id):
    count, width = rows.shape
    nb = width // B
    half = SLOTS * B // GROUPS // 2
    return pl.pallas_call(
        functools.partial(gram_kernel, nb),
        out_shape=jax.ShapeDtypeStruct((SLOTS * B, B), F32),
        in_specs=[pl.BlockSpec(memory_space=pltpu.VMEM)],
        out_specs=pl.BlockSpec(memory_space=pl.ANY),
        scratch_shapes=[
            pltpu.VMEM((width, count), BF),
            pltpu.VMEM((SLOTS * B, B), F32),
            pltpu.VMEM((GROUPS, half, B), F32),
            pltpu.VMEM((GROUPS, half, B), F32),
            pltpu.VMEM((GROUPS, 3, half // 4, B), F32),
            pltpu.VMEM((GROUPS, 3, half // 16, B), F32),
            pltpu.VMEM((GROUPS, 3, half // 64, B), F32),
            pltpu.VMEM((SLOTS * B, B), F32),
            pltpu.SemaphoreType.DMA((2, GROUPS)),
            pltpu.SemaphoreType.DMA((2, 3, GROUPS, 3)),
            pltpu.SemaphoreType.DMA((2, 3, GROUPS, 3)),
            pltpu.SemaphoreType.DMA((2, GROUPS)),
            pltpu.SemaphoreType.DMA,
        ],
        compiler_params=pltpu.CompilerParams(
            collective_id=collective_id, has_side_effects=True, vmem_limit_bytes=48 * 1024 * 1024),
        cost_estimate=pl.CostEstimate(flops=2 * count * width * width, bytes_accessed=100_000_000, transcendentals=0),
    )(rows)

def sketch_kernel(rank, w_hbm, turned_hbm, scale_ref, sketch_ref, weighted_ref, w, turned, part, relay, land, last,
                  w_sems, turned_sem, relay_sems, land_sems, last_sems):
    row, col = lax.axis_index("row"), lax.axis_index("col")
    coords = (col // 4, col % 4)
    lines = w.shape[3]
    width = turned.shape[0]

    def peer(axis, at):
        return (row, at * 4 + coords[1]) if axis == 0 else (row, coords[0] * 4 + at)

    def ahead(axis, step):
        return lax.rem(coords[axis] + step, 4)

    barrier = pltpu.get_barrier_semaphore()
    for axis in range(2):
        for step in range(1, 4):
            pl.semaphore_signal(barrier, inc=1, device_id=peer(axis, ahead(axis, step)), device_id_type=MESH)

    fetch_turned = pltpu.make_async_copy(turned_hbm, turned.at[pl.ds(0, rank), :], turned_sem)
    fetch_turned.start()
    fetches = {}
    order = [(side, step) for step in (2, 1, 3, 0) for side in range(2)]
    for side, step in order:
        at = ahead(side, step)
        fetches[side, step] = []
        for b in range(4):
            chunk = at * 4 + b if side == 0 else b * 4 + at
            copy = pltpu.make_async_copy(
                w_hbm.at[pl.ds(pl.multiple_of(chunk * 2 * lines + side * lines, 16), lines), :],
                w.at[side, at, b], w_sems.at[side, step, b])
            copy.start()
            fetches[side, step].append(copy)
    turned[rank:, :] = jnp.zeros((width - rank, turned.shape[1]), BF)
    fetch_turned.wait()

    def product(side, step):
        at = ahead(side, step)
        for copy in fetches[side, step]:
            copy.wait()

        def some(q, carry):
            cols = pl.ds(pl.multiple_of(q * 3 * B, B), 3 * B)
            result = lax.dot_general(
                w[side, at].reshape(4 * lines, w.shape[4]), turned[cols, :], (((1,), (1,)), ((), ())),
                preferred_element_type=F32)
            part[side, at, :, :, cols] = result.astype(BF).reshape(4, lines, 3 * B)
            return carry

        lax.fori_loop(0, width // (3 * B), some, 0)

    copies = []

    def push(src, dst, sems, index, device):
        copy = pltpu.make_async_remote_copy(
            src_ref=src, dst_ref=dst, send_sem=sems.at[(0,) + index], recv_sem=sems.at[(1,) + index],
            device_id=device, device_id_type=MESH)
        copy.start()
        copies.append(copy)
        return copy

    relays, lands = {}, {}
    for side, step in order:
        product(side, step)
        at = ahead(side, step)
        if (side, step) == (0, 2):
            pl.semaphore_wait(barrier, 6)
        if step == 2:
            for way, near in ((0, 1), (1, 3)):
                relays[side, way] = push(
                    part.at[side, at, pl.ds(2 * way, 2)], relay.at[side, way], relay_sems, (side, way),
                    peer(side, ahead(side, near)))
        elif step != 0:
            way = 0 if step == 1 else 1
            half = 1 - way
            lands[side, way, half] = push(
                part.at[side, at, pl.ds(2 * half, 2)], land.at[side, way, pl.ds(2 * half, 2)], land_sems,
                (side, way, half), peer(side, at))
    for side in range(2):
        for way, step in ((0, 1), (1, 3)):
            at = ahead(side, step)
            relays[side, way].wait_recv()
            for b in range(2):
                mine = part[side, at, 2 * way + b].astype(F32)
                part[side, at, 2 * way + b] = (mine + relay[side, way, b].astype(F32)).astype(BF)
            lands[side, way, way] = push(
                part.at[side, at, pl.ds(2 * way, 2)], land.at[side, way, pl.ds(2 * way, 2)], land_sems,
                (side, way, way), peer(side, at))
    lasts = {}
    for side in range(2):
        for way in range(2):
            for half in (1 - way, way):
                lands[side, way, half].wait_recv()
        for step in (2, 1, 3):
            at = ahead(1 - side, step)
            total = part[side, coords[side], at].astype(F32) + (
                land[side, 0, at].astype(F32) + land[side, 1, at].astype(F32))
            part[side, coords[side], at] = total.astype(BF)
            lasts[side, step] = push(
                part.at[side, coords[side], at], last.at[side, step - 1], last_sems, (side, step - 1),
                peer(1 - side, at))
    for side in range(2):
        at = coords[1 - side]
        total = part[side, coords[side], at].astype(F32) + (
            land[side, 0, at].astype(F32) + land[side, 1, at].astype(F32))
        for step in (1, 3, 2):
            lasts[side, step].wait_recv()
        total = total + ((last[side, 0].astype(F32) + last[side, 1].astype(F32)) + last[side, 2].astype(F32))
        mine = slice(side * lines, side * lines + lines)
        scale = scale_ref[mine, :]
        sketch = (scale * total).astype(BF)
        sketch_ref[mine, :] = sketch
        weighted_ref[mine, :] = (scale * sketch.astype(F32)).astype(BF)
    for copy in copies:
        copy.wait_send()


def sketch_rows(weight, test_matrix, own_scales, width, collective_id):
    block_rows, depth = weight.shape
    rank = test_matrix.shape[1]
    count = own_scales.shape[0]
    lines = count // 2
    result = jax.ShapeDtypeStruct((count, width), BF)
    vmem = pl.BlockSpec(memory_space=pltpu.VMEM)
    return pl.pallas_call(
        functools.partial(sketch_kernel, rank),
        out_shape=(result, result),
        in_specs=[pl.BlockSpec(memory_space=pl.ANY), pl.BlockSpec(memory_space=pl.ANY), vmem],
        out_specs=(vmem, vmem),
        scratch_shapes=[
            pltpu.VMEM((2, 4, 4, lines, depth), BF),
            pltpu.VMEM((width, depth), BF),
            pltpu.VMEM((2, 4, 4, lines, width), BF),
            pltpu.VMEM((2, 2, 2, lines, width), BF),
            pltpu.VMEM((2, 2, 4, lines, width), BF),
            pltpu.VMEM((2, 3, lines, width), BF),
            pltpu.SemaphoreType.DMA((2, 4, 4)),
            pltpu.SemaphoreType.DMA,
            pltpu.SemaphoreType.DMA((2, 2, 2)),
            pltpu.SemaphoreType.DMA((2, 2, 2, 2)),
            pltpu.SemaphoreType.DMA((2, 2, 3)),
        ],
        compiler_params=pltpu.CompilerParams(
            collective_id=collective_id, has_side_effects=True, vmem_limit_bytes=60 * 1024 * 1024),
        cost_estimate=pl.CostEstimate(flops=2 * block_rows * depth * width, bytes_accessed=100_000_000, transcendentals=0),
    )(weight, test_matrix.T, own_scales[:, None])


def factor_kernel(nb, rank, first, last, root_rows, root_cols, *refs):
    whole, whole_l = last == nb, root_rows is not None
    refs = list(refs)
    if first == 0:
        blocks_ref = refs.pop(0)
    else:
        work_in, linv_in, sum_in = refs.pop(0), refs.pop(0), refs.pop(0)
    rows_ref = refs.pop(0)
    if whole_l:
        values_ref, scale_ref = refs.pop(0), refs.pop(0)
        left_out, right_out = refs.pop(0), refs.pop(0)
    elif whole:
        result_ref = refs.pop(0)
    else:
        work_out, linv_out, sum_out = refs.pop(0), refs.pop(0), refs.pop(0)
    work, linv, left, right, column, lower = refs[:6]
    npad = nb * B
    wid = npad + 2 * B
    work[:, npad:] = jnp.zeros((npad, wid - npad), F32)
    right[:, npad:] = jnp.zeros((6 * B, wid - npad), BF)
    r0 = lax.broadcasted_iota(jnp.int32, (B, B), 0)
    r1 = lax.broadcasted_iota(jnp.int32, (B, B), 1)
    ri = lax.broadcasted_iota(jnp.int32, (npad, B), 0)
    if not whole_l:
        total = refs[6]

    def unpack(q):
        first, second = place(q, nb)
        block = blocks_ref[q * B:(q + 1) * B, :]
        if first == second == nb - 1:
            block = jnp.where((r0 == r1) & (r0 >= rank - (npad - B)), 1.0, block)
        a, b = slice(first * B, first * B + B), slice(second * B, second * B + B)
        work[a, b] = block
        if first != second:
            work[b, a] = block.T

    if first == 0:
        if not whole_l:
            total[...] = jnp.zeros_like(total)
        factor_inverse(blocks_ref[0:B, :], linv, [functools.partial(unpack, q) for q in range(nb * (nb + 1) // 2)])
    else:
        work[:, :npad] = work_in[...]
        linv[...] = linv_in[...]
        total[...] = sum_in[...]

    def two(ref, x):
        h = x.astype(BF)
        ref[:, :B] = h
        ref[:, B:] = (x - h.astype(F32)).astype(BF)

    def spread(j, rows, inv, diag):
        c = hdot(work[:, rows], inv, ((1,), (1,)))
        work[:, rows] = c
        below = ri >= j * B + B
        two(column, jnp.where(below, 0.0, c))
        if whole_l:
            two(lower, jnp.where(below, c, 0.0))
            own = jnp.where(r0 >= r1, hdot(diag, inv, ((1,), (1,))), 0.0)
            h = own.astype(BF)
            lower[rows, :B] = h
            lower[rows, B:] = (own - h.astype(F32)).astype(BF)
        return c

    def gather_up(j, rows):
        keep = B if j is not None else rank - (npad - B)
        x = jnp.dot(rows_ref[...], column[...], preferred_element_type=F32)
        x = x[:, :B] + x[:, B:]
        if whole_l:
            y = jnp.dot(values_ref[...], lower[...], preferred_element_type=F32)
            y = ((y[:, :B] + y[:, B:]) * (root_rows / scale_ref[...])).astype(BF)
            x = (root_cols * x).T.astype(BF)
            if j is None:
                left_out[:, npad - B:rank] = y[:, :keep]
                right_out[npad - B:rank, :] = x[:keep, :]
            else:
                left_out[:, rows] = y
                right_out[rows, :] = x
        else:
            x = x.astype(BF)
            total[...] += lax.dot_general(
                jnp.concatenate([x, x], axis=1), column[...], (((1,), (1,)), ((), ())),
                preferred_element_type=F32)

    def step(pieces, j, carry):
        rows = pl.ds(pl.multiple_of(j * B, B), B)
        after = pl.ds(pl.multiple_of(j * B + B, B), B)
        inv = linv[...]
        diag = work[rows, rows]
        next_u = hdot(inv, work[rows, after], ((1,), (0,)))
        next_c = hdot(work[after, rows], inv, ((1,), (1,)))
        next_diag = work[after, after] - hdot(next_c, next_u, ((1,), (0,)))

        def across():
            h, m, l = split3(hdot(inv, work[rows, :npad], ((1,), (0,))))
            for q, part in enumerate((h, m, h, m, l, h)):
                right[q * B:(q + 1) * B, :npad] = part
            work[rows, :] = jnp.zeros((B, wid), F32)
            work[rows, rows] = jnp.where(r0 == r1, 1.0, 0.0).astype(F32)

        def down():
            h, m, l = split3(spread(j, rows, inv, diag))
            for q, part in enumerate((h, h, m, m, h, l)):
                left[:, q * B:(q + 1) * B] = part

        def update(q):
            cols = pl.ds(pl.multiple_of(jnp.minimum((j + 1) * B + q * 2 * B, npad), B), 2 * B)
            work[:, cols] = work[:, cols] - jnp.dot(left[...], right[:, cols], preferred_element_type=F32)

        items = [across, down] + [functools.partial(update, q) for q in range(pieces)]
        items.append(functools.partial(gather_up, j, rows))
        factor_inverse(next_diag, linv, items)
        return carry

    early = nb // 2
    if first < early:
        lax.fori_loop(first, min(early, last), functools.partial(step, nb // 2), 0)
    if last > early:
        lax.fori_loop(max(first, early), min(last, nb - 1), functools.partial(step, (nb - early) // 2), 0)
    if not whole:
        work_out[...] = work[:, :npad]
        linv_out[...] = linv[...]
        sum_out[...] = total[...]
        return
    rows = slice(npad - B, npad)
    diag = work[rows, rows]
    work[rows, :] = jnp.zeros((B, wid), F32)
    work[rows, rows] = jnp.where(r0 == r1, 1.0, 0.0).astype(F32)
    spread(nb - 1, rows, linv[...], diag)
    gather_up(None, rows)
    if not whole_l:
        result_ref[...] = total[...].astype(BF)


def factor(operands, results, width, rank, first, last, root_rows=None, root_cols=None):
    nb = width // B
    vmem = pl.BlockSpec(memory_space=pltpu.VMEM)
    scratch = [
        pltpu.VMEM((width, width + 2 * B), F32),
        pltpu.VMEM((B, B), F32),
        pltpu.VMEM((width, 6 * B), BF),
        pltpu.VMEM((6 * B, width + 2 * B), BF),
        pltpu.VMEM((width, 2 * B), BF),
        pltpu.VMEM((width, 2 * B), BF),
    ]
    if root_rows is None:
        count = operands[-1].shape[0]
        scratch.append(pltpu.VMEM((count, width), F32))
    return pl.pallas_call(
        functools.partial(factor_kernel, nb, rank, first, last, root_rows, root_cols),
        out_shape=tuple(jax.ShapeDtypeStruct(shape, kind) for shape, kind in results),
        in_specs=[vmem] * len(operands),
        out_specs=(vmem,) * len(results),
        scratch_shapes=scratch,
        compiler_params=pltpu.CompilerParams(vmem_limit_bytes=56 * 1024 * 1024),
        cost_estimate=pl.CostEstimate(flops=20 * width**3, bytes_accessed=200_000_000, transcendentals=0),
    )(*operands)


def two_stage(blocks, rows, width, rank):
    count = rows.shape[0]
    half = width // B // 2
    state = factor(
        (blocks, rows), [((width, width), F32), ((B, B), F32), ((count, width), F32)], width, rank, 0, half)

    def finish(state):
        return factor((*state, rows), [((count, width), BF)], width, rank, half, width // B)[0]

    return state, finish


def per_device(weight, test_matrix, fisher):
    row_count = lax.axis_size("row")
    col_count = lax.axis_size("col")
    col_index = lax.axis_index("col")
    block_rows = weight.shape[0]
    slice_rows = block_rows // col_count
    total_rows = block_rows * row_count
    total_cols = weight.shape[1] * col_count
    rank = test_matrix.shape[1]
    width = -(-rank // B) * B
    scales = jnp.sqrt(fisher)
    own_scales = lax.dynamic_slice_in_dim(scales, col_index * slice_rows, slice_rows, 0)
    sketch, weighted_rows = sketch_rows(weight, test_matrix, own_scales, width, 3)
    weighted = lax.all_gather(weighted_rows, "col", axis=0, tiled=True)
    gram_one = gram_sum(sketch, 1)
    state, finish = two_stage(gram_one, sketch, width, rank)
    weighted, state = lax.optimization_barrier((weighted, state))
    combos = lax.psum_scatter(
        lax.dot_general(
            weight, weighted, (((0,), (0,)), ((), ())), preferred_element_type=F32
        ).astype(BF),
        "row",
        scatter_dimension=0,
        tiled=True,
    ).astype(BF)
    projected = finish(state)
    combos, projected = lax.optimization_barrier((combos, projected))
    all_combos = lax.all_gather(combos, "row", axis=0, tiled=True)
    gram_two = gram_sum(combos, 2)
    left_factor, right_turned = factor(
        (gram_two, all_combos, projected, own_scales[:, None]),
        [((slice_rows, rank), BF), ((rank, weight.shape[1]), BF)],
        width, rank, 0, width // B, math.sqrt(total_rows), math.sqrt(total_cols),
    )
    return (left_factor, right_turned.T)


def solution(mesh):
    return jax.shard_map(
        per_device,
        mesh=mesh,
        in_specs=(P("row", "col"), P("col", None), P("row")),
        out_specs=(P(("row", "col"), None), P("col", None)),
        check_vma=False,
    )
```

```python
import functools
import math

import jax
import jax.numpy as jnp
from jax import lax
from jax.experimental import pallas as pl
from jax.experimental.pallas import tpu as pltpu
from jax.sharding import PartitionSpec as P

F32 = jnp.float32
BF = jnp.bfloat16
B = 128

def factor_inverse(block, out_ref, others=()):
    groups = B // 8
    sub = lax.broadcasted_iota(jnp.int32, (8, B), 0)
    lane = lax.broadcasted_iota(jnp.int32, (8, B), 1)
    rows = [block[8 * t: 8 * t + 8, :] for t in range(groups)]
    inv = [jnp.where(lane == sub + 8 * t, 1.0, 0.0).astype(F32) for t in range(groups)]
    given = 0
    for p in range(groups):
        while given < len(others) and given * groups <= p * len(others):
            others[given]()
            given += 1
        c0 = 8 * p
        cols = [[jnp.broadcast_to(rows[t][:, c0 + j: c0 + j + 1], (8, B)) for j in range(8)]
                for t in range(p, groups)]
        panel, wide = rows[p], inv[p]
        arow, wrow = [], []
        for j in range(8):
            own = cols[0][j]
            rinv = lax.rsqrt(jnp.broadcast_to(own[j:j + 1, :], (8, B)))
            for t in range(groups - p):
                cols[t][j] = cols[t][j] * rinv
            own = cols[0][j]
            for k in range(j + 1, 8):
                fac = jnp.broadcast_to(own[k:k + 1, :], (8, B))
                for t in range(groups - p):
                    cols[t][k] = cols[t][k] - cols[t][j] * fac
            ar = jnp.broadcast_to(panel[j:j + 1, :], (8, B)) * rinv
            wr = jnp.broadcast_to(wide[j:j + 1, :], (8, B)) * rinv
            arow.append(ar)
            wrow.append(wr)
            below = jnp.where(sub > j, own, 0.0)
            panel = panel - below * ar
            wide = jnp.where(sub == j, wr, wide - below * wr)
        inv[p] = wide
        for t in range(p + 1, groups):
            a, w = rows[t], inv[t]
            for j in range(8):
                a = a - cols[t - p][j] * arow[j]
                w = w - cols[t - p][j] * wrow[j]
            rows[t], inv[t] = a, w
    for item in others[given:]:
        item()
    for t in range(groups):
        out_ref[8 * t: 8 * t + 8, :] = inv[t]

def split3(x):
    h = x.astype(BF)
    r = x - h.astype(F32)
    m = r.astype(BF)
    l = (r - m.astype(F32)).astype(BF)
    return h, m, l

def hdot(a, b, dims):
    return lax.dot_general(a, b, (dims, ((), ())), precision=lax.Precision.HIGHEST, preferred_element_type=F32)


SLOTS = 48
PARTS = 1
GROUPS = 3
MESH = pl.DeviceIdType.MESH


def place(q, nb):
    first = q % nb
    return first, (first + q // nb) % nb


def gram_kernel(nb, rows_ref, out_ref, turned, packed, core_in, acc, in_one, in_two, in_three, total,
                core_sems, ring_sems, back_sems, core_back, out_sem):
    row, col = lax.axis_index("row"), lax.axis_index("col")
    z, core, x, y = row // 2, row % 2, col // 4, col % 4
    coords = (x, y, z)

    def peer(axis, at):
        if axis == 0:
            return (row, at * 4 + y)
        if axis == 1:
            return (row, x * 4 + at)
        return (at * 2 + core, col)

    other = (z * 2 + 1 - core, col)
    barrier = pltpu.get_barrier_semaphore()
    pl.semaphore_signal(barrier, inc=1, device_id=other, device_id_type=MESH)
    for axis in range(3):
        for step in range(1, 4):
            pl.semaphore_signal(barrier, inc=1, device_id=peer(axis, (coords[axis] + step) % 4), device_id_type=MESH)

    turned[...] = rows_ref[...].astype(F32).T.astype(BF)

    used = nb * (nb + 1) // 2
    for first in range(nb):
        strip = jnp.dot(turned[first * B:first * B + B, :], rows_ref[...], preferred_element_type=F32)
        for step in range((nb + 1) // 2):
            q, second = step * nb + first, (first + step) % nb
            packed[q * B:(q + 1) * B, :] = strip[:, second * B:(second + 1) * B]
    packed[used * B:, :] = jnp.zeros(((SLOTS - used) * B, B), F32)
    pl.semaphore_wait(barrier, 10)

    per = SLOTS * B // GROUPS
    half = per // 2

    def push(src, dst, sems, index, device):
        copy = pltpu.make_async_remote_copy(
            src_ref=src, dst_ref=dst, send_sem=sems.at[(0,) + index], recv_sem=sems.at[(1,) + index],
            device_id=device, device_id_type=MESH)
        copy.start()
        return copy

    def core_push(g):
        away = pl.multiple_of(g * per + (1 - core) * half, half)
        return push(packed.at[pl.ds(away, half), :], core_in.at[g], core_sems, (g,), other)

    copies = [core_push(g) for g in range(GROUPS)]
    for g in range(GROUPS):
        copies[g].wait()
        keep = pl.multiple_of(g * per + core * half, half)
        acc[g] = packed[pl.ds(keep, half), :] + core_in[g]
    size = half
    starts = [0] * GROUPS
    for phase, landing in enumerate((in_one, in_two, in_three)):
        size //= 4
        copies = []
        for g in range(GROUPS):
            axis = (g + phase) % 3
            copies.append([
                push(acc.at[g, pl.ds(pl.multiple_of(starts[g] + (coords[axis] + step) % 4 * size, size), size), :],
                     landing.at[g, step - 1], ring_sems, (phase, g, step - 1),
                     peer(axis, (coords[axis] + step) % 4))
                for step in range(1, 4)])
        for g in range(GROUPS):
            axis = (g + phase) % 3
            starts[g] = pl.multiple_of(starts[g] + coords[axis] * size, size)
            for copy in copies[g]:
                copy.wait()
            mine = pl.ds(starts[g], size)
            acc[g, mine, :] = (acc[g, mine, :] + landing[g, 0]) + (landing[g, 1] + landing[g, 2])
    bases = []
    for g in range(GROUPS):
        base = pl.multiple_of(g * per + core * half, half)
        bases.append(base)
        total[pl.ds(pl.multiple_of(base + starts[g], size), size), :] = acc[g, pl.ds(starts[g], size), :]
    for phase in (2, 1, 0):
        copies = []
        for g in range(GROUPS):
            axis = (g + phase) % 3
            span = total.at[pl.ds(pl.multiple_of(bases[g] + starts[g], size), size), :]
            copies.append([
                push(span, span, back_sems, (phase, g, step - 1), peer(axis, (coords[axis] + step) % 4))
                for step in range(1, 4)])
        for g in range(GROUPS):
            axis = (g + phase) % 3
            starts[g] = starts[g] - coords[axis] * size
            for copy in copies[g]:
                copy.wait()
        size *= 4
    copies = []
    for g in range(GROUPS):
        span = total.at[pl.ds(bases[g], half), :]
        copies.append(push(span, span, core_back, (g,), other))
    for copy in copies:
        copy.wait()
    final = pltpu.make_async_copy(total, out_ref, out_sem)
    final.start()
    final.wait()


def gram_sum(rows, collective_id):
    count, width = rows.shape
    nb = width // B
    half = SLOTS * B // GROUPS // 2
    return pl.pallas_call(
        functools.partial(gram_kernel, nb),
        out_shape=jax.ShapeDtypeStruct((SLOTS * B, B), F32),
        in_specs=[pl.BlockSpec(memory_space=pltpu.VMEM)],
        out_specs=pl.BlockSpec(memory_space=pl.ANY),
        scratch_shapes=[
            pltpu.VMEM((width, count), BF),
            pltpu.VMEM((SLOTS * B, B), F32),
            pltpu.VMEM((GROUPS, half, B), F32),
            pltpu.VMEM((GROUPS, half, B), F32),
            pltpu.VMEM((GROUPS, 3, half // 4, B), F32),
            pltpu.VMEM((GROUPS, 3, half // 16, B), F32),
            pltpu.VMEM((GROUPS, 3, half // 64, B), F32),
            pltpu.VMEM((SLOTS * B, B), F32),
            pltpu.SemaphoreType.DMA((2, GROUPS)),
            pltpu.SemaphoreType.DMA((2, 3, GROUPS, 3)),
            pltpu.SemaphoreType.DMA((2, 3, GROUPS, 3)),
            pltpu.SemaphoreType.DMA((2, GROUPS)),
            pltpu.SemaphoreType.DMA,
        ],
        compiler_params=pltpu.CompilerParams(
            collective_id=collective_id, has_side_effects=True, vmem_limit_bytes=24 * 1024 * 1024),
        cost_estimate=pl.CostEstimate(flops=2 * count * width * width, bytes_accessed=100_000_000, transcendentals=0),
    )(rows)

def sketch_kernel(rank, w_hbm, turned_hbm, scale_ref, sketch_ref, weighted_ref, w, turned, part, relay, land, last,
                  w_sems, turned_sem, relay_sems, land_sems, last_sems):
    row, col = lax.axis_index("row"), lax.axis_index("col")
    coords = (col // 4, col % 4)
    lines = w.shape[3]
    width = turned.shape[0]

    def peer(axis, at):
        return (row, at * 4 + coords[1]) if axis == 0 else (row, coords[0] * 4 + at)

    def ahead(axis, step):
        return lax.rem(coords[axis] + step, 4)

    barrier = pltpu.get_barrier_semaphore()
    for axis in range(2):
        for step in range(1, 4):
            pl.semaphore_signal(barrier, inc=1, device_id=peer(axis, ahead(axis, step)), device_id_type=MESH)

    fetch_turned = pltpu.make_async_copy(turned_hbm, turned.at[pl.ds(0, rank), :], turned_sem)
    fetch_turned.start()
    fetches = {}
    order = [(side, step) for step in (2, 1, 3, 0) for side in range(2)]
    for side, step in order:
        at = ahead(side, step)
        fetches[side, step] = []
        for b in range(4):
            chunk = at * 4 + b if side == 0 else b * 4 + at
            copy = pltpu.make_async_copy(
                w_hbm.at[pl.ds(pl.multiple_of(chunk * 2 * lines + side * lines, 16), lines), :],
                w.at[side, at, b], w_sems.at[side, step, b])
            copy.start()
            fetches[side, step].append(copy)
    turned[rank:, :] = jnp.zeros((width - rank, turned.shape[1]), BF)
    fetch_turned.wait()

    def product(side, step):
        at = ahead(side, step)
        for copy in fetches[side, step]:
            copy.wait()

        def some(q, carry):
            cols = pl.ds(pl.multiple_of(q * 3 * B, B), 3 * B)
            result = lax.dot_general(
                w[side, at].reshape(4 * lines, w.shape[4]), turned[cols, :], (((1,), (1,)), ((), ())),
                preferred_element_type=F32)
            part[side, at, :, :, cols] = result.astype(BF).reshape(4, lines, 3 * B)
            return carry

        lax.fori_loop(0, width // (3 * B), some, 0)

    copies = []

    def push(src, dst, sems, index, device):
        copy = pltpu.make_async_remote_copy(
            src_ref=src, dst_ref=dst, send_sem=sems.at[(0,) + index], recv_sem=sems.at[(1,) + index],
            device_id=device, device_id_type=MESH)
        copy.start()
        copies.append(copy)
        return copy

    relays, lands = {}, {}
    for side, step in order:
        product(side, step)
        at = ahead(side, step)
        if (side, step) == (0, 2):
            pl.semaphore_wait(barrier, 6)
        if step == 2:
            for way, near in ((0, 1), (1, 3)):
                relays[side, way] = push(
                    part.at[side, at, pl.ds(2 * way, 2)], relay.at[side, way], relay_sems, (side, way),
                    peer(side, ahead(side, near)))
        elif step != 0:
            way = 0 if step == 1 else 1
            half = 1 - way
            lands[side, way, half] = push(
                part.at[side, at, pl.ds(2 * half, 2)], land.at[side, way, pl.ds(2 * half, 2)], land_sems,
                (side, way, half), peer(side, at))
    for side in range(2):
        for way, step in ((0, 1), (1, 3)):
            at = ahead(side, step)
            relays[side, way].wait_recv()
            for b in range(2):
                mine = part[side, at, 2 * way + b].astype(F32)
                part[side, at, 2 * way + b] = (mine + relay[side, way, b].astype(F32)).astype(BF)
            lands[side, way, way] = push(
                part.at[side, at, pl.ds(2 * way, 2)], land.at[side, way, pl.ds(2 * way, 2)], land_sems,
                (side, way, way), peer(side, at))
    lasts = {}
    for side in range(2):
        for way in range(2):
            for half in (1 - way, way):
                lands[side, way, half].wait_recv()
        for step in (2, 1, 3):
            at = ahead(1 - side, step)
            total = part[side, coords[side], at].astype(F32) + (
                land[side, 0, at].astype(F32) + land[side, 1, at].astype(F32))
            part[side, coords[side], at] = total.astype(BF)
            lasts[side, step] = push(
                part.at[side, coords[side], at], last.at[side, step - 1], last_sems, (side, step - 1),
                peer(1 - side, at))
    for side in range(2):
        at = coords[1 - side]
        total = part[side, coords[side], at].astype(F32) + (
            land[side, 0, at].astype(F32) + land[side, 1, at].astype(F32))
        for step in (1, 3, 2):
            lasts[side, step].wait_recv()
        total = total + ((last[side, 0].astype(F32) + last[side, 1].astype(F32)) + last[side, 2].astype(F32))
        mine = slice(side * lines, side * lines + lines)
        scale = scale_ref[mine, :]
        sketch = (scale * total).astype(BF)
        sketch_ref[mine, :] = sketch
        weighted_ref[mine, :] = (scale * sketch.astype(F32)).astype(BF)
    for copy in copies:
        copy.wait_send()


def sketch_rows(weight, test_matrix, own_scales, width, collective_id):
    block_rows, depth = weight.shape
    rank = test_matrix.shape[1]
    count = own_scales.shape[0]
    lines = count // 2
    result = jax.ShapeDtypeStruct((count, width), BF)
    vmem = pl.BlockSpec(memory_space=pltpu.VMEM)
    return pl.pallas_call(
        functools.partial(sketch_kernel, rank),
        out_shape=(result, result),
        in_specs=[pl.BlockSpec(memory_space=pl.ANY), pl.BlockSpec(memory_space=pl.ANY), vmem],
        out_specs=(vmem, vmem),
        scratch_shapes=[
            pltpu.VMEM((2, 4, 4, lines, depth), BF),
            pltpu.VMEM((width, depth), BF),
            pltpu.VMEM((2, 4, 4, lines, width), BF),
            pltpu.VMEM((2, 2, 2, lines, width), BF),
            pltpu.VMEM((2, 2, 4, lines, width), BF),
            pltpu.VMEM((2, 3, lines, width), BF),
            pltpu.SemaphoreType.DMA((2, 4, 4)),
            pltpu.SemaphoreType.DMA,
            pltpu.SemaphoreType.DMA((2, 2, 2)),
            pltpu.SemaphoreType.DMA((2, 2, 2, 2)),
            pltpu.SemaphoreType.DMA((2, 2, 3)),
        ],
        compiler_params=pltpu.CompilerParams(
            collective_id=collective_id, has_side_effects=True, vmem_limit_bytes=48 * 1024 * 1024),
        cost_estimate=pl.CostEstimate(flops=2 * block_rows * depth * width, bytes_accessed=100_000_000, transcendentals=0),
    )(weight, test_matrix.T, own_scales[:, None])


def factor_kernel(nb, rank, first, last, root_rows, root_cols, *refs):
    whole, whole_l = last == nb, root_rows is not None
    refs = list(refs)
    if first == 0:
        blocks_ref = refs.pop(0)
    else:
        work_in, linv_in, sum_in = refs.pop(0), refs.pop(0), refs.pop(0)
    rows_ref = refs.pop(0)
    if whole_l:
        values_ref, scale_ref = refs.pop(0), refs.pop(0)
        left_out, right_out = refs.pop(0), refs.pop(0)
    elif whole:
        result_ref = refs.pop(0)
    else:
        work_out, linv_out, sum_out = refs.pop(0), refs.pop(0), refs.pop(0)
    work, linv, left, right, column, lower = refs[:6]
    npad = nb * B
    wid = npad + 2 * B
    work[:, npad:] = jnp.zeros((npad, wid - npad), F32)
    right[:, npad:] = jnp.zeros((6 * B, wid - npad), BF)
    r0 = lax.broadcasted_iota(jnp.int32, (B, B), 0)
    r1 = lax.broadcasted_iota(jnp.int32, (B, B), 1)
    ri = lax.broadcasted_iota(jnp.int32, (npad, B), 0)
    if not whole_l:
        total = refs[6]

    def unpack(q):
        first, second = place(q, nb)
        block = blocks_ref[q * B:(q + 1) * B, :]
        if first == second == nb - 1:
            block = jnp.where((r0 == r1) & (r0 >= rank - (npad - B)), 1.0, block)
        a, b = slice(first * B, first * B + B), slice(second * B, second * B + B)
        work[a, b] = block
        if first != second:
            work[b, a] = block.T

    if first == 0:
        if not whole_l:
            total[...] = jnp.zeros_like(total)
        factor_inverse(blocks_ref[0:B, :], linv, [functools.partial(unpack, q) for q in range(nb * (nb + 1) // 2)])
    else:
        work[:, :npad] = work_in[...]
        linv[...] = linv_in[...]
        total[...] = sum_in[...]

    def two(ref, x):
        h = x.astype(BF)
        ref[:, :B] = h
        ref[:, B:] = (x - h.astype(F32)).astype(BF)

    def spread(j, rows, inv, diag):
        c = hdot(work[:, rows], inv, ((1,), (1,)))
        work[:, rows] = c
        below = ri >= j * B + B
        two(column, jnp.where(below, 0.0, c))
        if whole_l:
            two(lower, jnp.where(below, c, 0.0))
            own = jnp.where(r0 >= r1, hdot(diag, inv, ((1,), (1,))), 0.0)
            h = own.astype(BF)
            lower[rows, :B] = h
            lower[rows, B:] = (own - h.astype(F32)).astype(BF)
        return c

    def gather_up(j, rows):
        keep = B if j is not None else rank - (npad - B)
        x = jnp.dot(rows_ref[...], column[...], preferred_element_type=F32)
        x = x[:, :B] + x[:, B:]
        if whole_l:
            y = jnp.dot(values_ref[...], lower[...], preferred_element_type=F32)
            y = ((y[:, :B] + y[:, B:]) * (root_rows / scale_ref[...])).astype(BF)
            x = (root_cols * x).T.astype(BF)
            if j is None:
                left_out[:, npad - B:rank] = y[:, :keep]
                right_out[npad - B:rank, :] = x[:keep, :]
            else:
                left_out[:, rows] = y
                right_out[rows, :] = x
        else:
            x = x.astype(BF)
            total[...] += lax.dot_general(
                jnp.concatenate([x, x], axis=1), column[...], (((1,), (1,)), ((), ())),
                preferred_element_type=F32)

    def step(pieces, j, carry):
        rows = pl.ds(pl.multiple_of(j * B, B), B)
        after = pl.ds(pl.multiple_of(j * B + B, B), B)
        inv = linv[...]
        diag = work[rows, rows]
        next_u = hdot(inv, work[rows, after], ((1,), (0,)))
        next_c = hdot(work[after, rows], inv, ((1,), (1,)))
        next_diag = work[after, after] - hdot(next_c, next_u, ((1,), (0,)))

        def across():
            h, m, l = split3(hdot(inv, work[rows, :npad], ((1,), (0,))))
            for q, part in enumerate((h, m, h, m, l, h)):
                right[q * B:(q + 1) * B, :npad] = part
            work[rows, :] = jnp.zeros((B, wid), F32)
            work[rows, rows] = jnp.where(r0 == r1, 1.0, 0.0).astype(F32)

        def down():
            h, m, l = split3(spread(j, rows, inv, diag))
            for q, part in enumerate((h, h, m, m, h, l)):
                left[:, q * B:(q + 1) * B] = part

        def update(q):
            cols = pl.ds(pl.multiple_of(jnp.minimum((j + 1) * B + q * 2 * B, npad), B), 2 * B)
            work[:, cols] = work[:, cols] - jnp.dot(left[...], right[:, cols], preferred_element_type=F32)

        items = [across, down] + [functools.partial(update, q) for q in range(pieces)]
        items.append(functools.partial(gather_up, j, rows))
        factor_inverse(next_diag, linv, items)
        return carry

    early = nb // 2
    if first < early:
        lax.fori_loop(first, min(early, last), functools.partial(step, nb // 2), 0)
    if last > early:
        lax.fori_loop(max(first, early), min(last, nb - 1), functools.partial(step, (nb - early) // 2), 0)
    if not whole:
        work_out[...] = work[:, :npad]
        linv_out[...] = linv[...]
        sum_out[...] = total[...]
        return
    rows = slice(npad - B, npad)
    diag = work[rows, rows]
    work[rows, :] = jnp.zeros((B, wid), F32)
    work[rows, rows] = jnp.where(r0 == r1, 1.0, 0.0).astype(F32)
    spread(nb - 1, rows, linv[...], diag)
    gather_up(None, rows)
    if not whole_l:
        result_ref[...] = total[...].astype(BF)


def factor(operands, results, width, rank, first, last, root_rows=None, root_cols=None):
    nb = width // B
    vmem = pl.BlockSpec(memory_space=pltpu.VMEM)
    scratch = [
        pltpu.VMEM((width, width + 2 * B), F32),
        pltpu.VMEM((B, B), F32),
        pltpu.VMEM((width, 6 * B), BF),
        pltpu.VMEM((6 * B, width + 2 * B), BF),
        pltpu.VMEM((width, 2 * B), BF),
        pltpu.VMEM((width, 2 * B), BF),
    ]
    if root_rows is None:
        count = operands[-1].shape[0]
        scratch.append(pltpu.VMEM((count, width), F32))
    return pl.pallas_call(
        functools.partial(factor_kernel, nb, rank, first, last, root_rows, root_cols),
        out_shape=tuple(jax.ShapeDtypeStruct(shape, kind) for shape, kind in results),
        in_specs=[vmem] * len(operands),
        out_specs=(vmem,) * len(results),
        scratch_shapes=scratch,
        compiler_params=pltpu.CompilerParams(vmem_limit_bytes=36 * 1024 * 1024),
        cost_estimate=pl.CostEstimate(flops=20 * width**3, bytes_accessed=200_000_000, transcendentals=0),
    )(*operands)


def two_stage(blocks, rows, width, rank):
    count = rows.shape[0]
    half = 3
    state = factor(
        (blocks, rows), [((width, width), F32), ((B, B), F32), ((count, width), F32)], width, rank, 0, half)

    def finish(state):
        return factor((*state, rows), [((count, width), BF)], width, rank, half, width // B)[0]

    return state, finish


def per_device(weight, test_matrix, fisher):
    row_count = lax.axis_size("row")
    col_count = lax.axis_size("col")
    col_index = lax.axis_index("col")
    block_rows = weight.shape[0]
    slice_rows = block_rows // col_count
    total_rows = block_rows * row_count
    total_cols = weight.shape[1] * col_count
    rank = test_matrix.shape[1]
    width = -(-rank // B) * B
    scales = jnp.sqrt(fisher)
    own_scales = lax.dynamic_slice_in_dim(scales, col_index * slice_rows, slice_rows, 0)
    sketch, weighted_rows = sketch_rows(weight, test_matrix, own_scales, width, 3)
    weighted = lax.all_gather(weighted_rows, "col", axis=0, tiled=True)
    gram_one = gram_sum(sketch, 1)
    state, finish = two_stage(gram_one, sketch, width, rank)
    weighted, state = lax.optimization_barrier((weighted, state))
    combos = lax.psum_scatter(
        lax.dot_general(
            weighted, weight, (((0,), (0,)), ((), ())), preferred_element_type=F32
        ).astype(BF).T,
        "row",
        scatter_dimension=0,
        tiled=True,
    ).astype(BF)
    projected = finish(state)
    combos, projected = lax.optimization_barrier((combos, projected))
    all_combos = lax.all_gather(combos, "row", axis=0, tiled=True)
    gram_two = gram_sum(combos, 2)
    left_factor, right_turned = factor(
        (gram_two, all_combos, projected, own_scales[:, None]),
        [((slice_rows, rank), BF), ((rank, weight.shape[1]), BF)],
        width, rank, 0, width // B, math.sqrt(total_rows), math.sqrt(total_cols),
    )
    return (left_factor, right_turned.T)


def solution(mesh):
    return jax.shard_map(
        per_device,
        mesh=mesh,
        in_specs=(P("row", "col"), P("col", None), P("row")),
        out_specs=(P(("row", "col"), None), P("col", None)),
        check_vma=False,
    )
```

```python
import functools
import math

import jax
import jax.numpy as jnp
from jax import lax
from jax.experimental import pallas as pl
from jax.experimental.pallas import tpu as pltpu
from jax.sharding import PartitionSpec as P

F32 = jnp.float32
BF = jnp.bfloat16
B = 128

def factor_inverse(block, out_ref, others=(), used=B):
    groups = used // 8
    sub = lax.broadcasted_iota(jnp.int32, (8, B), 0)
    lane = lax.broadcasted_iota(jnp.int32, (8, B), 1)
    rows = [block[8 * t: 8 * t + 8, :] for t in range(groups)]
    inv = [jnp.where(lane == sub + 8 * t, 1.0, 0.0).astype(F32) for t in range(groups)]
    given = 0
    for p in range(groups):
        while given < len(others) and given * groups <= p * len(others):
            others[given]()
            given += 1
        c0 = 8 * p
        cols = [[jnp.broadcast_to(rows[t][:, c0 + j: c0 + j + 1], (8, B)) for j in range(8)]
                for t in range(p, groups)]
        panel, wide = rows[p], inv[p]
        arow, wrow = [], []
        for j in range(8):
            own = cols[0][j]
            rinv = lax.rsqrt(jnp.broadcast_to(own[j:j + 1, :], (8, B)))
            for t in range(groups - p):
                cols[t][j] = cols[t][j] * rinv
            own = cols[0][j]
            for k in range(j + 1, 8):
                fac = jnp.broadcast_to(own[k:k + 1, :], (8, B))
                for t in range(groups - p):
                    cols[t][k] = cols[t][k] - cols[t][j] * fac
            ar = jnp.broadcast_to(panel[j:j + 1, :], (8, B)) * rinv
            wr = jnp.broadcast_to(wide[j:j + 1, :], (8, B)) * rinv
            arow.append(ar)
            wrow.append(wr)
            below = jnp.where(sub > j, own, 0.0)
            panel = panel - below * ar
            wide = jnp.where(sub == j, wr, wide - below * wr)
        inv[p] = wide
        for t in range(p + 1, groups):
            a, w = rows[t], inv[t]
            for j in range(8):
                a = a - cols[t - p][j] * arow[j]
                w = w - cols[t - p][j] * wrow[j]
            rows[t], inv[t] = a, w
    for item in others[given:]:
        item()
    for t in range(groups):
        out_ref[8 * t: 8 * t + 8, :] = inv[t]
    if used < B:
        r = lax.broadcasted_iota(jnp.int32, (B - used, B), 0)
        c = lax.broadcasted_iota(jnp.int32, (B - used, B), 1)
        out_ref[used:, :] = jnp.where(r + used == c, 1.0, 0.0).astype(F32)

def split3(x):
    h = x.astype(BF)
    r = x - h.astype(F32)
    m = r.astype(BF)
    l = (r - m.astype(F32)).astype(BF)
    return h, m, l

def hdot(a, b, dims):
    return lax.dot_general(a, b, (dims, ((), ())), precision=lax.Precision.HIGHEST, preferred_element_type=F32)


SLOTS = 48
PARTS = 1
GROUPS = 3
MESH = pl.DeviceIdType.MESH


def place(q, nb):
    first = q % nb
    return first, (first + q // nb) % nb


def gram_kernel(nb, rows_ref, out_ref, turned, packed, core_in, acc, in_one, in_two, in_three, total,
                core_sems, ring_sems, back_sems, core_back, out_sem):
    row, col = lax.axis_index("row"), lax.axis_index("col")
    z, core, x, y = row // 2, row % 2, col // 4, col % 4
    coords = (x, y, z)

    def peer(axis, at):
        if axis == 0:
            return (row, at * 4 + y)
        if axis == 1:
            return (row, x * 4 + at)
        return (at * 2 + core, col)

    other = (z * 2 + 1 - core, col)
    barrier = pltpu.get_barrier_semaphore()
    pl.semaphore_signal(barrier, inc=1, device_id=other, device_id_type=MESH)
    for axis in range(3):
        for step in range(1, 4):
            pl.semaphore_signal(barrier, inc=1, device_id=peer(axis, (coords[axis] + step) % 4), device_id_type=MESH)

    turned[...] = rows_ref[...].astype(F32).T.astype(BF)

    used = nb * (nb + 1) // 2
    for first in range(nb):
        strip = jnp.dot(turned[first * B:first * B + B, :], rows_ref[...], preferred_element_type=F32)
        for step in range((nb + 1) // 2):
            q, second = step * nb + first, (first + step) % nb
            packed[q * B:(q + 1) * B, :] = strip[:, second * B:(second + 1) * B]
    packed[used * B:, :] = jnp.zeros(((SLOTS - used) * B, B), F32)
    pl.semaphore_wait(barrier, 10)

    per = SLOTS * B // GROUPS
    half = per // 2

    def push(src, dst, sems, index, device):
        copy = pltpu.make_async_remote_copy(
            src_ref=src, dst_ref=dst, send_sem=sems.at[(0,) + index], recv_sem=sems.at[(1,) + index],
            device_id=device, device_id_type=MESH)
        copy.start()
        return copy

    def core_push(g):
        away = pl.multiple_of(g * per + (1 - core) * half, half)
        return push(packed.at[pl.ds(away, half), :], core_in.at[g], core_sems, (g,), other)

    copies = [core_push(g) for g in range(GROUPS)]
    for g in range(GROUPS):
        copies[g].wait()
        keep = pl.multiple_of(g * per + core * half, half)
        acc[g] = packed[pl.ds(keep, half), :] + core_in[g]
    size = half
    starts = [0] * GROUPS
    for phase, landing in enumerate((in_one, in_two, in_three)):
        size //= 4
        copies = []
        for g in range(GROUPS):
            axis = (g + phase) % 3
            copies.append([
                push(acc.at[g, pl.ds(pl.multiple_of(starts[g] + (coords[axis] + step) % 4 * size, size), size), :],
                     landing.at[g, step - 1], ring_sems, (phase, g, step - 1),
                     peer(axis, (coords[axis] + step) % 4))
                for step in range(1, 4)])
        for g in range(GROUPS):
            axis = (g + phase) % 3
            starts[g] = pl.multiple_of(starts[g] + coords[axis] * size, size)
            for copy in copies[g]:
                copy.wait()
            mine = pl.ds(starts[g], size)
            acc[g, mine, :] = (acc[g, mine, :] + landing[g, 0]) + (landing[g, 1] + landing[g, 2])
    bases = []
    for g in range(GROUPS):
        base = pl.multiple_of(g * per + core * half, half)
        bases.append(base)
        total[pl.ds(pl.multiple_of(base + starts[g], size), size), :] = acc[g, pl.ds(starts[g], size), :]
    for phase in (2, 1, 0):
        copies = []
        for g in range(GROUPS):
            axis = (g + phase) % 3
            span = total.at[pl.ds(pl.multiple_of(bases[g] + starts[g], size), size), :]
            copies.append([
                push(span, span, back_sems, (phase, g, step - 1), peer(axis, (coords[axis] + step) % 4))
                for step in range(1, 4)])
        for g in range(GROUPS):
            axis = (g + phase) % 3
            starts[g] = starts[g] - coords[axis] * size
            for copy in copies[g]:
                copy.wait()
        size *= 4
    copies = []
    for g in range(GROUPS):
        span = total.at[pl.ds(bases[g], half), :]
        copies.append(push(span, span, core_back, (g,), other))
    for copy in copies:
        copy.wait()
    final = pltpu.make_async_copy(total, out_ref, out_sem)
    final.start()
    final.wait()


def gram_sum(rows, collective_id):
    count, width = rows.shape
    nb = width // B
    half = SLOTS * B // GROUPS // 2
    return pl.pallas_call(
        functools.partial(gram_kernel, nb),
        out_shape=jax.ShapeDtypeStruct((SLOTS * B, B), F32),
        in_specs=[pl.BlockSpec(memory_space=pltpu.VMEM)],
        out_specs=pl.BlockSpec(memory_space=pl.ANY),
        scratch_shapes=[
            pltpu.VMEM((width, count), BF),
            pltpu.VMEM((SLOTS * B, B), F32),
            pltpu.VMEM((GROUPS, half, B), F32),
            pltpu.VMEM((GROUPS, half, B), F32),
            pltpu.VMEM((GROUPS, 3, half // 4, B), F32),
            pltpu.VMEM((GROUPS, 3, half // 16, B), F32),
            pltpu.VMEM((GROUPS, 3, half // 64, B), F32),
            pltpu.VMEM((SLOTS * B, B), F32),
            pltpu.SemaphoreType.DMA((2, GROUPS)),
            pltpu.SemaphoreType.DMA((2, 3, GROUPS, 3)),
            pltpu.SemaphoreType.DMA((2, 3, GROUPS, 3)),
            pltpu.SemaphoreType.DMA((2, GROUPS)),
            pltpu.SemaphoreType.DMA,
        ],
        compiler_params=pltpu.CompilerParams(
            collective_id=collective_id, has_side_effects=True, vmem_limit_bytes=20 * 1024 * 1024),
        cost_estimate=pl.CostEstimate(flops=2 * count * width * width, bytes_accessed=100_000_000, transcendentals=0),
    )(rows)

def sketch_kernel(rank, w_hbm, turned_hbm, scale_ref, sketch_ref, weighted_ref, w, turned, part, relay, land, last,
                  w_sems, turned_sem, relay_sems, land_sems, last_sems):
    row, col = lax.axis_index("row"), lax.axis_index("col")
    coords = (col // 4, col % 4)
    lines = w.shape[3]
    width = turned.shape[0]

    def peer(axis, at):
        return (row, at * 4 + coords[1]) if axis == 0 else (row, coords[0] * 4 + at)

    def ahead(axis, step):
        return lax.rem(coords[axis] + step, 4)

    barrier = pltpu.get_barrier_semaphore()
    for axis in range(2):
        for step in range(1, 4):
            pl.semaphore_signal(barrier, inc=1, device_id=peer(axis, ahead(axis, step)), device_id_type=MESH)

    fetch_turned = pltpu.make_async_copy(turned_hbm, turned.at[pl.ds(0, rank), :], turned_sem)
    fetch_turned.start()
    fetches = {}
    order = [(side, step) for step in (2, 1, 3, 0) for side in range(2)]
    for side, step in order:
        at = ahead(side, step)
        fetches[side, step] = []
        for b in range(4):
            chunk = at * 4 + b if side == 0 else b * 4 + at
            copy = pltpu.make_async_copy(
                w_hbm.at[pl.ds(pl.multiple_of(chunk * 2 * lines + side * lines, 16), lines), :],
                w.at[side, at, b], w_sems.at[side, step, b])
            copy.start()
            fetches[side, step].append(copy)
    turned[rank:, :] = jnp.zeros((width - rank, turned.shape[1]), BF)
    fetch_turned.wait()

    def product(side, step):
        at = ahead(side, step)
        for copy in fetches[side, step]:
            copy.wait()

        def some(q, carry):
            cols = pl.ds(pl.multiple_of(q * 3 * B, B), 3 * B)
            result = lax.dot_general(
                w[side, at].reshape(4 * lines, w.shape[4]), turned[cols, :], (((1,), (1,)), ((), ())),
                preferred_element_type=F32)
            part[side, at, :, :, cols] = result.astype(BF).reshape(4, lines, 3 * B)
            return carry

        lax.fori_loop(0, width // (3 * B), some, 0)

    copies = []

    def push(src, dst, sems, index, device):
        copy = pltpu.make_async_remote_copy(
            src_ref=src, dst_ref=dst, send_sem=sems.at[(0,) + index], recv_sem=sems.at[(1,) + index],
            device_id=device, device_id_type=MESH)
        copy.start()
        copies.append(copy)
        return copy

    relays, lands = {}, {}
    for side, step in order:
        product(side, step)
        at = ahead(side, step)
        if (side, step) == (0, 2):
            pl.semaphore_wait(barrier, 6)
        if step == 2:
            for way, near in ((0, 1), (1, 3)):
                relays[side, way] = push(
                    part.at[side, at, pl.ds(2 * way, 2)], relay.at[side, way], relay_sems, (side, way),
                    peer(side, ahead(side, near)))
        elif step != 0:
            way = 0 if step == 1 else 1
            half = 1 - way
            lands[side, way, half] = push(
                part.at[side, at, pl.ds(2 * half, 2)], land.at[side, way, pl.ds(2 * half, 2)], land_sems,
                (side, way, half), peer(side, at))
    for side in range(2):
        for way, step in ((0, 1), (1, 3)):
            at = ahead(side, step)
            relays[side, way].wait_recv()
            for b in range(2):
                mine = part[side, at, 2 * way + b].astype(F32)
                part[side, at, 2 * way + b] = (mine + relay[side, way, b].astype(F32)).astype(BF)
            lands[side, way, way] = push(
                part.at[side, at, pl.ds(2 * way, 2)], land.at[side, way, pl.ds(2 * way, 2)], land_sems,
                (side, way, way), peer(side, at))
    lasts = {}
    for side in range(2):
        for way in range(2):
            for half in (1 - way, way):
                lands[side, way, half].wait_recv()
        for step in (2, 1, 3):
            at = ahead(1 - side, step)
            total = part[side, coords[side], at].astype(F32) + (
                land[side, 0, at].astype(F32) + land[side, 1, at].astype(F32))
            part[side, coords[side], at] = total.astype(BF)
            lasts[side, step] = push(
                part.at[side, coords[side], at], last.at[side, step - 1], last_sems, (side, step - 1),
                peer(1 - side, at))
    for side in range(2):
        at = coords[1 - side]
        total = part[side, coords[side], at].astype(F32) + (
            land[side, 0, at].astype(F32) + land[side, 1, at].astype(F32))
        for step in (1, 3, 2):
            lasts[side, step].wait_recv()
        total = total + ((last[side, 0].astype(F32) + last[side, 1].astype(F32)) + last[side, 2].astype(F32))
        mine = slice(side * lines, side * lines + lines)
        scale = scale_ref[mine, :]
        sketch = (scale * total).astype(BF)
        sketch_ref[mine, :] = sketch
        weighted_ref[mine, :] = (scale * sketch.astype(F32)).astype(BF)
    for copy in copies:
        copy.wait_send()


def sketch_rows(weight, test_matrix, own_scales, width, collective_id):
    block_rows, depth = weight.shape
    rank = test_matrix.shape[1]
    count = own_scales.shape[0]
    lines = count // 2
    result = jax.ShapeDtypeStruct((count, width), BF)
    vmem = pl.BlockSpec(memory_space=pltpu.VMEM)
    return pl.pallas_call(
        functools.partial(sketch_kernel, rank),
        out_shape=(result, result),
        in_specs=[pl.BlockSpec(memory_space=pl.ANY), pl.BlockSpec(memory_space=pl.ANY), vmem],
        out_specs=(vmem, vmem),
        scratch_shapes=[
            pltpu.VMEM((2, 4, 4, lines, depth), BF),
            pltpu.VMEM((width, depth), BF),
            pltpu.VMEM((2, 4, 4, lines, width), BF),
            pltpu.VMEM((2, 2, 2, lines, width), BF),
            pltpu.VMEM((2, 2, 4, lines, width), BF),
            pltpu.VMEM((2, 3, lines, width), BF),
            pltpu.SemaphoreType.DMA((2, 4, 4)),
            pltpu.SemaphoreType.DMA,
            pltpu.SemaphoreType.DMA((2, 2, 2)),
            pltpu.SemaphoreType.DMA((2, 2, 2, 2)),
            pltpu.SemaphoreType.DMA((2, 2, 3)),
        ],
        compiler_params=pltpu.CompilerParams(
            collective_id=collective_id, has_side_effects=True, vmem_limit_bytes=46 * 1024 * 1024),
        cost_estimate=pl.CostEstimate(flops=2 * block_rows * depth * width, bytes_accessed=100_000_000, transcendentals=0),
    )(weight, test_matrix.T, own_scales[:, None])


def factor_kernel(nb, rank, first, last, root_rows, root_cols, *refs):
    whole, whole_l = last == nb, root_rows is not None
    refs = list(refs)
    if first == 0:
        blocks_ref = refs.pop(0)
    else:
        work_in, linv_in, sum_in = refs.pop(0), refs.pop(0), refs.pop(0)
    rows_ref = refs.pop(0)
    if whole_l:
        values_ref, scale_ref = refs.pop(0), refs.pop(0)
        left_out, right_out = refs.pop(0), refs.pop(0)
    elif whole:
        result_ref = refs.pop(0)
    else:
        work_out, linv_out, sum_out = refs.pop(0), refs.pop(0), refs.pop(0)
    work, linv, left, right, column, lower = refs[:6]
    npad = nb * B
    wid = npad + 2 * B
    work[:, npad:] = jnp.zeros((npad, wid - npad), F32)
    right[:, npad:] = jnp.zeros((6 * B, wid - npad), BF)
    r0 = lax.broadcasted_iota(jnp.int32, (B, B), 0)
    r1 = lax.broadcasted_iota(jnp.int32, (B, B), 1)
    ri = lax.broadcasted_iota(jnp.int32, (npad, B), 0)
    if not whole_l:
        total = refs[6]

    def unpack(q):
        first, second = place(q, nb)
        block = blocks_ref[q * B:(q + 1) * B, :]
        if first == second == nb - 1:
            block = jnp.where((r0 == r1) & (r0 >= rank - (npad - B)), 1.0, block)
        a, b = slice(first * B, first * B + B), slice(second * B, second * B + B)
        work[a, b] = block
        if first != second:
            work[b, a] = block.T

    if first == 0:
        if not whole_l:
            total[...] = jnp.zeros_like(total)
        factor_inverse(blocks_ref[0:B, :], linv, [functools.partial(unpack, q) for q in range(nb * (nb + 1) // 2)])
    else:
        work[:, :first * B] = jnp.zeros((npad, first * B), F32)
        work[:, first * B:npad] = work_in[...]
        linv[...] = linv_in[...]
        total[...] = sum_in[...]

    def spread(j, rows, inv, diag):
        c = hdot(work[:, rows], inv, ((1,), (1,)))
        work[:, rows] = c
        below = ri >= j * B + B
        if whole_l:
            column[:, :B] = jnp.where(below, 0.0, c).astype(BF)
            lower[...] = jnp.where(below, c, 0.0).astype(BF)
            lower[rows, :] = jnp.where(r0 >= r1, hdot(diag, inv, ((1,), (1,))), 0.0).astype(BF)
        else:
            h, m, unused = split3(jnp.where(below, 0.0, c))
            column[:, :B] = h
            column[:, B:] = m
        return c

    def gather_up(j, rows):
        keep = B if j is not None else rank - (npad - B)
        if whole_l:
            x = jnp.dot(rows_ref[...], column[:, :B], preferred_element_type=F32)
            y = jnp.dot(values_ref[...], lower[...], preferred_element_type=F32)
            y = (y * (root_rows / scale_ref[...])).astype(BF)
            x = (root_cols * x).T.astype(BF)
            if j is None:
                left_out[:, npad - B:rank] = y[:, :keep]
                right_out[npad - B:rank, :] = x[:keep, :]
            else:
                left_out[:, rows] = y
                right_out[rows, :] = x
        else:
            x = jnp.dot(rows_ref[...], column[...], preferred_element_type=F32)
            x = (x[:, :B] + x[:, B:]).astype(BF)
            total[...] += lax.dot_general(
                jnp.concatenate([x, x], axis=1), column[...], (((1,), (1,)), ((), ())),
                preferred_element_type=F32)

    def step(pieces, used, j, carry):
        rows = pl.ds(pl.multiple_of(j * B, B), B)
        after = pl.ds(pl.multiple_of(j * B + B, B), B)
        inv = linv[...]
        diag = work[rows, rows]
        next_u = hdot(inv, work[rows, after], ((1,), (0,)))
        next_c = hdot(work[after, rows], inv, ((1,), (1,)))
        next_diag = work[after, after] - hdot(next_c, next_u, ((1,), (0,)))

        def across():
            h, m, l = split3(hdot(inv, work[rows, :npad], ((1,), (0,))))
            for q, part in enumerate((h, m, h, m, l, h)):
                right[q * B:(q + 1) * B, :npad] = part
            work[rows, :] = jnp.zeros((B, wid), F32)
            work[rows, rows] = jnp.where(r0 == r1, 1.0, 0.0).astype(F32)

        def down():
            h, m, l = split3(spread(j, rows, inv, diag))
            for q, part in enumerate((h, h, m, m, h, l)):
                left[:, q * B:(q + 1) * B] = part

        def update(q):
            cols = pl.ds(pl.multiple_of(jnp.minimum((j + 1) * B + q * 2 * B, npad), B), 2 * B)
            work[:, cols] = work[:, cols] - jnp.dot(left[...], right[:, cols], preferred_element_type=F32)

        items = [across, down] + [functools.partial(update, q) for q in range(pieces)]
        items.append(functools.partial(gather_up, j, rows))
        factor_inverse(next_diag, linv, items, used)
        return carry

    tail = -(-(rank - (npad - B)) // 8) * 8
    for start in range(first, min(last, nb - 2), 2):
        stop = min(start + 2, last, nb - 2)
        lax.fori_loop(start, stop, functools.partial(step, (nb - start) // 2, B), 0)
    if whole:
        lax.fori_loop(nb - 2, nb - 1, functools.partial(step, 1, tail), 0)
    if not whole:
        work_out[...] = work[:, last * B:npad]
        linv_out[...] = linv[...]
        sum_out[...] = total[...]
        return
    rows = slice(npad - B, npad)
    diag = work[rows, rows]
    work[rows, :] = jnp.zeros((B, wid), F32)
    work[rows, rows] = jnp.where(r0 == r1, 1.0, 0.0).astype(F32)
    spread(nb - 1, rows, linv[...], diag)
    gather_up(None, rows)
    if not whole_l:
        result_ref[...] = total[...].astype(BF)


def factor(operands, results, width, rank, first, last, root_rows=None, root_cols=None):
    nb = width // B
    vmem = pl.BlockSpec(memory_space=pltpu.VMEM)
    scratch = [
        pltpu.VMEM((width, width + 2 * B), F32),
        pltpu.VMEM((B, B), F32),
        pltpu.VMEM((width, 6 * B), BF),
        pltpu.VMEM((6 * B, width + 2 * B), BF),
        pltpu.VMEM((width, 2 * B), BF),
        pltpu.VMEM((width, B), BF),
    ]
    if root_rows is None:
        count = operands[-1].shape[0]
        scratch.append(pltpu.VMEM((count, width), F32))
    return pl.pallas_call(
        functools.partial(factor_kernel, nb, rank, first, last, root_rows, root_cols),
        out_shape=tuple(jax.ShapeDtypeStruct(shape, kind) for shape, kind in results),
        in_specs=[vmem] * len(operands),
        out_specs=(vmem,) * len(results),
        scratch_shapes=scratch,
        compiler_params=pltpu.CompilerParams(vmem_limit_bytes=30 * 1024 * 1024),
        cost_estimate=pl.CostEstimate(flops=20 * width**3, bytes_accessed=200_000_000, transcendentals=0),
    )(*operands)


def two_stage(blocks, rows, width, rank):
    count = rows.shape[0]
    half = 3
    state = factor(
        (blocks, rows), [((width, width - half * B), F32), ((B, B), F32), ((count, width), F32)], width, rank, 0, half)

    def finish(state):
        return factor((*state, rows), [((count, width), BF)], width, rank, half, width // B)[0]

    return state, finish


def per_device(weight, test_matrix, fisher):
    row_count = lax.axis_size("row")
    col_count = lax.axis_size("col")
    col_index = lax.axis_index("col")
    block_rows = weight.shape[0]
    slice_rows = block_rows // col_count
    total_rows = block_rows * row_count
    total_cols = weight.shape[1] * col_count
    rank = test_matrix.shape[1]
    width = -(-rank // B) * B
    scales = jnp.sqrt(fisher)
    own_scales = lax.dynamic_slice_in_dim(scales, col_index * slice_rows, slice_rows, 0)
    sketch, weighted_rows = sketch_rows(weight, test_matrix, own_scales, width, 3)
    weighted = lax.all_gather(weighted_rows, "col", axis=0, tiled=True)
    gram_one = gram_sum(sketch, 1)
    state, finish = two_stage(gram_one, sketch, width, rank)
    weighted, state = lax.optimization_barrier((weighted, state))
    combos = lax.psum_scatter(
        lax.dot_general(
            weighted, weight, (((0,), (0,)), ((), ())), preferred_element_type=F32
        ).astype(BF).T,
        "row",
        scatter_dimension=0,
        tiled=True,
    ).astype(BF)
    projected = finish(state)
    combos, projected = lax.optimization_barrier((combos, projected))
    all_combos = lax.all_gather(combos, "row", axis=0, tiled=True)
    gram_two = gram_sum(combos, 2)
    left_factor, right_turned = factor(
        (gram_two, all_combos, projected, own_scales[:, None]),
        [((slice_rows, rank), BF), ((rank, weight.shape[1]), BF)],
        width, rank, 0, width // B, math.sqrt(total_rows), math.sqrt(total_cols),
    )
    return (left_factor, right_turned.T)


def solution(mesh):
    return jax.shard_map(
        per_device,
        mesh=mesh,
        in_specs=(P("row", "col"), P("col", None), P("row")),
        out_specs=(P(("row", "col"), None), P("col", None)),
        check_vma=False,
    )
```

```python
import functools
import math

import jax
import jax.numpy as jnp
from jax import lax
from jax.experimental import pallas as pl
from jax.experimental.pallas import tpu as pltpu
from jax.sharding import PartitionSpec as P

F32 = jnp.float32
BF = jnp.bfloat16
B = 128

def factor_inverse(block, out_ref, others=(), used=B):
    groups = used // 8
    sub = lax.broadcasted_iota(jnp.int32, (8, B), 0)
    lane = lax.broadcasted_iota(jnp.int32, (8, B), 1)
    rows = [block[8 * t: 8 * t + 8, :] for t in range(groups)]
    inv = [jnp.where(lane == sub + 8 * t, 1.0, 0.0).astype(F32) for t in range(groups)]
    given = 0
    for p in range(groups):
        while given < len(others) and given * groups <= p * len(others):
            others[given]()
            given += 1
        c0 = 8 * p
        cols = [[jnp.broadcast_to(rows[t][:, c0 + j: c0 + j + 1], (8, B)) for j in range(8)]
                for t in range(p, groups)]
        panel, wide = rows[p], inv[p]
        arow, wrow = [], []
        for j in range(8):
            own = cols[0][j]
            rinv = lax.rsqrt(jnp.broadcast_to(own[j:j + 1, :], (8, B)))
            for t in range(groups - p):
                cols[t][j] = cols[t][j] * rinv
            own = cols[0][j]
            for k in range(j + 1, 8):
                fac = jnp.broadcast_to(own[k:k + 1, :], (8, B))
                for t in range(groups - p):
                    cols[t][k] = cols[t][k] - cols[t][j] * fac
            ar = jnp.broadcast_to(panel[j:j + 1, :], (8, B)) * rinv
            wr = jnp.broadcast_to(wide[j:j + 1, :], (8, B)) * rinv
            arow.append(ar)
            wrow.append(wr)
            below = jnp.where(sub > j, own, 0.0)
            panel = panel - below * ar
            wide = jnp.where(sub == j, wr, wide - below * wr)
        inv[p] = wide
        for t in range(p + 1, groups):
            a, w = rows[t], inv[t]
            for j in range(8):
                a = a - cols[t - p][j] * arow[j]
                w = w - cols[t - p][j] * wrow[j]
            rows[t], inv[t] = a, w
    for item in others[given:]:
        item()
    for t in range(groups):
        out_ref[8 * t: 8 * t + 8, :] = inv[t]
    if used < B:
        r = lax.broadcasted_iota(jnp.int32, (B - used, B), 0)
        c = lax.broadcasted_iota(jnp.int32, (B - used, B), 1)
        out_ref[used:, :] = jnp.where(r + used == c, 1.0, 0.0).astype(F32)

def split3(x):
    h = x.astype(BF)
    r = x - h.astype(F32)
    m = r.astype(BF)
    l = (r - m.astype(F32)).astype(BF)
    return h, m, l

def hdot(a, b, dims):
    return lax.dot_general(a, b, (dims, ((), ())), precision=lax.Precision.HIGHEST, preferred_element_type=F32)


SLOTS = 48
PARTS = 1
GROUPS = 3
MESH = pl.DeviceIdType.MESH


def place(q, nb):
    first = q % nb
    return first, (first + q // nb) % nb


def gram_kernel(nb, rows_ref, out_ref, turned, packed, core_in, acc, in_one, in_two, in_three, total,
                core_sems, ring_sems, back_sems, core_back, out_sem):
    row, col = lax.axis_index("row"), lax.axis_index("col")
    z, core, x, y = row // 2, row % 2, col // 4, col % 4
    coords = (x, y, z)

    def peer(axis, at):
        if axis == 0:
            return (row, at * 4 + y)
        if axis == 1:
            return (row, x * 4 + at)
        return (at * 2 + core, col)

    other = (z * 2 + 1 - core, col)
    barrier = pltpu.get_barrier_semaphore()
    pl.semaphore_signal(barrier, inc=1, device_id=other, device_id_type=MESH)
    for axis in range(3):
        for step in range(1, 4):
            pl.semaphore_signal(barrier, inc=1, device_id=peer(axis, (coords[axis] + step) % 4), device_id_type=MESH)

    turned[...] = rows_ref[...].astype(F32).T.astype(BF)

    used = nb * (nb + 1) // 2
    for first in range(nb):
        strip = jnp.dot(turned[first * B:first * B + B, :], rows_ref[...], preferred_element_type=F32)
        for step in range((nb + 1) // 2):
            q, second = step * nb + first, (first + step) % nb
            packed[q * B:(q + 1) * B, :] = strip[:, second * B:(second + 1) * B]
    packed[used * B:, :] = jnp.zeros(((SLOTS - used) * B, B), F32)
    pl.semaphore_wait(barrier, 10)

    per = SLOTS * B // GROUPS
    half = per // 2

    def push(src, dst, sems, index, device):
        copy = pltpu.make_async_remote_copy(
            src_ref=src, dst_ref=dst, send_sem=sems.at[(0,) + index], recv_sem=sems.at[(1,) + index],
            device_id=device, device_id_type=MESH)
        copy.start()
        return copy

    def core_push(g):
        away = pl.multiple_of(g * per + (1 - core) * half, half)
        return push(packed.at[pl.ds(away, half), :], core_in.at[g], core_sems, (g,), other)

    copies = [core_push(g) for g in range(GROUPS)]
    for g in range(GROUPS):
        copies[g].wait()
        keep = pl.multiple_of(g * per + core * half, half)
        acc[g] = packed[pl.ds(keep, half), :] + core_in[g]
    size = half
    starts = [0] * GROUPS
    for phase, landing in enumerate((in_one, in_two, in_three)):
        size //= 4
        copies = []
        for g in range(GROUPS):
            axis = (g + phase) % 3
            copies.append([
                push(acc.at[g, pl.ds(pl.multiple_of(starts[g] + (coords[axis] + step) % 4 * size, size), size), :],
                     landing.at[g, step - 1], ring_sems, (phase, g, step - 1),
                     peer(axis, (coords[axis] + step) % 4))
                for step in range(1, 4)])
        for g in range(GROUPS):
            axis = (g + phase) % 3
            starts[g] = pl.multiple_of(starts[g] + coords[axis] * size, size)
            for copy in copies[g]:
                copy.wait()
            mine = pl.ds(starts[g], size)
            acc[g, mine, :] = (acc[g, mine, :] + landing[g, 0]) + (landing[g, 1] + landing[g, 2])
    bases = []
    for g in range(GROUPS):
        base = pl.multiple_of(g * per + core * half, half)
        bases.append(base)
        total[pl.ds(pl.multiple_of(base + starts[g], size), size), :] = acc[g, pl.ds(starts[g], size), :]
    for phase in (2, 1, 0):
        copies = []
        for g in range(GROUPS):
            axis = (g + phase) % 3
            span = total.at[pl.ds(pl.multiple_of(bases[g] + starts[g], size), size), :]
            copies.append([
                push(span, span, back_sems, (phase, g, step - 1), peer(axis, (coords[axis] + step) % 4))
                for step in range(1, 4)])
        for g in range(GROUPS):
            axis = (g + phase) % 3
            starts[g] = starts[g] - coords[axis] * size
            for copy in copies[g]:
                copy.wait()
        size *= 4
    copies = []
    for g in range(GROUPS):
        span = total.at[pl.ds(bases[g], half), :]
        copies.append(push(span, span, core_back, (g,), other))
    for copy in copies:
        copy.wait()
    final = pltpu.make_async_copy(total, out_ref, out_sem)
    final.start()
    final.wait()


def gram_sum(rows, collective_id):
    count, width = rows.shape
    nb = width // B
    half = SLOTS * B // GROUPS // 2
    return pl.pallas_call(
        functools.partial(gram_kernel, nb),
        out_shape=jax.ShapeDtypeStruct((SLOTS * B, B), F32),
        in_specs=[pl.BlockSpec(memory_space=pltpu.VMEM)],
        out_specs=pl.BlockSpec(memory_space=pl.ANY),
        scratch_shapes=[
            pltpu.VMEM((width, count), BF),
            pltpu.VMEM((SLOTS * B, B), F32),
            pltpu.VMEM((GROUPS, half, B), F32),
            pltpu.VMEM((GROUPS, half, B), F32),
            pltpu.VMEM((GROUPS, 3, half // 4, B), F32),
            pltpu.VMEM((GROUPS, 3, half // 16, B), F32),
            pltpu.VMEM((GROUPS, 3, half // 64, B), F32),
            pltpu.VMEM((SLOTS * B, B), F32),
            pltpu.SemaphoreType.DMA((2, GROUPS)),
            pltpu.SemaphoreType.DMA((2, 3, GROUPS, 3)),
            pltpu.SemaphoreType.DMA((2, 3, GROUPS, 3)),
            pltpu.SemaphoreType.DMA((2, GROUPS)),
            pltpu.SemaphoreType.DMA,
        ],
        compiler_params=pltpu.CompilerParams(
            collective_id=collective_id, has_side_effects=True, vmem_limit_bytes=20 * 1024 * 1024),
        cost_estimate=pl.CostEstimate(flops=2 * count * width * width, bytes_accessed=100_000_000, transcendentals=0),
    )(rows)

def sketch_kernel(rank, w_hbm, turned_hbm, scale_ref, sketch_ref, weighted_ref, w, turned, part, relay, land, last,
                  w_sems, turned_sem, relay_sems, land_sems, last_sems):
    row, col = lax.axis_index("row"), lax.axis_index("col")
    coords = (col // 4, col % 4)
    lines = w.shape[3]
    width = turned.shape[0]

    def peer(axis, at):
        return (row, at * 4 + coords[1]) if axis == 0 else (row, coords[0] * 4 + at)

    def ahead(axis, step):
        return lax.rem(coords[axis] + step, 4)

    barrier = pltpu.get_barrier_semaphore()
    for axis in range(2):
        for step in range(1, 4):
            pl.semaphore_signal(barrier, inc=1, device_id=peer(axis, ahead(axis, step)), device_id_type=MESH)

    fetch_turned = pltpu.make_async_copy(turned_hbm, turned.at[pl.ds(0, rank), :], turned_sem)
    fetch_turned.start()
    fetches = {}
    order = [(side, step) for step in (2, 1, 3, 0) for side in range(2)]
    for side, step in order:
        at = ahead(side, step)
        fetches[side, step] = []
        for b in range(4):
            chunk = at * 4 + b if side == 0 else b * 4 + at
            copy = pltpu.make_async_copy(
                w_hbm.at[pl.ds(pl.multiple_of(chunk * 2 * lines + side * lines, 16), lines), :],
                w.at[side, at, b], w_sems.at[side, step, b])
            copy.start()
            fetches[side, step].append(copy)
    turned[rank:, :] = jnp.zeros((width - rank, turned.shape[1]), BF)
    fetch_turned.wait()

    def product(side, step, start=0, count=4):
        at = ahead(side, step)
        for copy in fetches[side, step][start:start + count]:
            copy.wait()

        def some(q, carry):
            cols = pl.ds(pl.multiple_of(q * 3 * B, B), 3 * B)
            result = lax.dot_general(
                w[side, at, start:start + count].reshape(count * lines, w.shape[4]), turned[cols, :],
                (((1,), (1,)), ((), ())), preferred_element_type=F32)
            part[side, at, start:start + count, :, cols] = result.astype(BF).reshape(count, lines, 3 * B)
            return carry

        lax.fori_loop(0, width // (3 * B), some, 0)

    copies = []

    def push(src, dst, sems, index, device):
        copy = pltpu.make_async_remote_copy(
            src_ref=src, dst_ref=dst, send_sem=sems.at[(0,) + index], recv_sem=sems.at[(1,) + index],
            device_id=device, device_id_type=MESH)
        copy.start()
        copies.append(copy)
        return copy

    relays, lands = {}, {}
    for way, near in ((0, 1), (1, 3)):
        for side in range(2):
            product(side, 2, 2 * way, 2)
            if (way, side) == (0, 0):
                pl.semaphore_wait(barrier, 6)
            relays[side, way] = push(
                part.at[side, ahead(side, 2), pl.ds(2 * way, 2)], relay.at[side, way], relay_sems, (side, way),
                peer(side, ahead(side, near)))
    for side, step in order[2:]:
        product(side, step)
        at = ahead(side, step)
        if step != 0:
            way = 0 if step == 1 else 1
            half = 1 - way
            lands[side, way, half] = push(
                part.at[side, at, pl.ds(2 * half, 2)], land.at[side, way, pl.ds(2 * half, 2)], land_sems,
                (side, way, half), peer(side, at))
    for side in range(2):
        for way, step in ((0, 1), (1, 3)):
            at = ahead(side, step)
            relays[side, way].wait_recv()
            for b in range(2):
                mine = part[side, at, 2 * way + b].astype(F32)
                part[side, at, 2 * way + b] = (mine + relay[side, way, b].astype(F32)).astype(BF)
            lands[side, way, way] = push(
                part.at[side, at, pl.ds(2 * way, 2)], land.at[side, way, pl.ds(2 * way, 2)], land_sems,
                (side, way, way), peer(side, at))
    lasts = {}
    for side in range(2):
        for way in range(2):
            for half in (1 - way, way):
                lands[side, way, half].wait_recv()
        for step in (2, 1, 3):
            at = ahead(1 - side, step)
            total = part[side, coords[side], at].astype(F32) + (
                land[side, 0, at].astype(F32) + land[side, 1, at].astype(F32))
            part[side, coords[side], at] = total.astype(BF)
            lasts[side, step] = push(
                part.at[side, coords[side], at], last.at[side, step - 1], last_sems, (side, step - 1),
                peer(1 - side, at))
    for side in range(2):
        at = coords[1 - side]
        total = part[side, coords[side], at].astype(F32) + (
            land[side, 0, at].astype(F32) + land[side, 1, at].astype(F32))
        for step in (1, 3, 2):
            lasts[side, step].wait_recv()
        total = total + ((last[side, 0].astype(F32) + last[side, 1].astype(F32)) + last[side, 2].astype(F32))
        mine = slice(side * lines, side * lines + lines)
        scale = scale_ref[mine, :]
        sketch = (scale * total).astype(BF)
        sketch_ref[mine, :] = sketch
        weighted_ref[mine, :] = (scale * sketch.astype(F32)).astype(BF)
    for copy in copies:
        copy.wait_send()


def sketch_rows(weight, test_matrix, own_scales, width, collective_id):
    block_rows, depth = weight.shape
    rank = test_matrix.shape[1]
    count = own_scales.shape[0]
    lines = count // 2
    result = jax.ShapeDtypeStruct((count, width), BF)
    vmem = pl.BlockSpec(memory_space=pltpu.VMEM)
    return pl.pallas_call(
        functools.partial(sketch_kernel, rank),
        out_shape=(result, result),
        in_specs=[pl.BlockSpec(memory_space=pl.ANY), pl.BlockSpec(memory_space=pl.ANY), vmem],
        out_specs=(vmem, vmem),
        scratch_shapes=[
            pltpu.VMEM((2, 4, 4, lines, depth), BF),
            pltpu.VMEM((width, depth), BF),
            pltpu.VMEM((2, 4, 4, lines, width), BF),
            pltpu.VMEM((2, 2, 2, lines, width), BF),
            pltpu.VMEM((2, 2, 4, lines, width), BF),
            pltpu.VMEM((2, 3, lines, width), BF),
            pltpu.SemaphoreType.DMA((2, 4, 4)),
            pltpu.SemaphoreType.DMA,
            pltpu.SemaphoreType.DMA((2, 2, 2)),
            pltpu.SemaphoreType.DMA((2, 2, 2, 2)),
            pltpu.SemaphoreType.DMA((2, 2, 3)),
        ],
        compiler_params=pltpu.CompilerParams(
            collective_id=collective_id, has_side_effects=True, vmem_limit_bytes=46 * 1024 * 1024),
        cost_estimate=pl.CostEstimate(flops=2 * block_rows * depth * width, bytes_accessed=100_000_000, transcendentals=0),
    )(weight, test_matrix.T, own_scales[:, None])


def factor_kernel(nb, rank, first, last, root_rows, root_cols, *refs):
    whole, whole_l = last == nb, root_rows is not None
    refs = list(refs)
    if first == 0:
        blocks_ref = refs.pop(0)
    else:
        work_in, linv_in, sum_in = refs.pop(0), refs.pop(0), refs.pop(0)
    rows_ref = refs.pop(0)
    if whole_l:
        values_ref, scale_ref = refs.pop(0), refs.pop(0)
        left_out, right_out = refs.pop(0), refs.pop(0)
    elif whole:
        result_ref = refs.pop(0)
    else:
        work_out, linv_out, sum_out = refs.pop(0), refs.pop(0), refs.pop(0)
    work, linv, left, right, column, lower = refs[:6]
    npad = nb * B
    wid = npad + 2 * B
    work[:, npad:] = jnp.zeros((npad, wid - npad), F32)
    right[:, npad:] = jnp.zeros((6 * B, wid - npad), BF)
    r0 = lax.broadcasted_iota(jnp.int32, (B, B), 0)
    r1 = lax.broadcasted_iota(jnp.int32, (B, B), 1)
    ri = lax.broadcasted_iota(jnp.int32, (npad, B), 0)
    if not whole_l:
        total = refs[6]

    def unpack(q):
        first, second = place(q, nb)
        block = blocks_ref[q * B:(q + 1) * B, :]
        if first == second == nb - 1:
            block = jnp.where((r0 == r1) & (r0 >= rank - (npad - B)), 1.0, block)
        a, b = slice(first * B, first * B + B), slice(second * B, second * B + B)
        work[a, b] = block
        if first != second:
            work[b, a] = block.T

    if first == 0:
        if not whole_l:
            total[...] = jnp.zeros_like(total)
        factor_inverse(blocks_ref[0:B, :], linv, [functools.partial(unpack, q) for q in range(nb * (nb + 1) // 2)])
    else:
        work[:, :first * B] = jnp.zeros((npad, first * B), F32)
        work[:, first * B:npad] = work_in[...]
        linv[...] = linv_in[...]
        total[...] = sum_in[...]

    def spread(j, rows, inv, diag):
        c = hdot(work[:, rows], inv, ((1,), (1,)))
        work[:, rows] = c
        below = ri >= j * B + B
        if whole_l:
            column[:, :B] = jnp.where(below, 0.0, c).astype(BF)
            lower[...] = jnp.where(below, c, 0.0).astype(BF)
            lower[rows, :] = jnp.where(r0 >= r1, hdot(diag, inv, ((1,), (1,))), 0.0).astype(BF)
        else:
            h, m, unused = split3(jnp.where(below, 0.0, c))
            column[:, :B] = h
            column[:, B:] = m
        return c

    def gather_up(j, rows):
        keep = B if j is not None else rank - (npad - B)
        if whole_l:
            x = jnp.dot(rows_ref[...], column[:, :B], preferred_element_type=F32)
            y = jnp.dot(values_ref[...], lower[...], preferred_element_type=F32)
            y = (y * (root_rows / scale_ref[...])).astype(BF)
            x = (root_cols * x).T.astype(BF)
            if j is None:
                left_out[:, npad - B:rank] = y[:, :keep]
                right_out[npad - B:rank, :] = x[:keep, :]
            else:
                left_out[:, rows] = y
                right_out[rows, :] = x
        else:
            x = jnp.dot(rows_ref[...], column[...], preferred_element_type=F32)
            x = (x[:, :B] + x[:, B:]).astype(BF)
            total[...] += lax.dot_general(
                jnp.concatenate([x, x], axis=1), column[...], (((1,), (1,)), ((), ())),
                preferred_element_type=F32)

    def step(pieces, used, j, carry):
        rows = pl.ds(pl.multiple_of(j * B, B), B)
        after = pl.ds(pl.multiple_of(j * B + B, B), B)
        inv = linv[...]
        diag = work[rows, rows]
        next_u = hdot(inv, work[rows, after], ((1,), (0,)))
        next_c = hdot(work[after, rows], inv, ((1,), (1,)))
        next_diag = work[after, after] - hdot(next_c, next_u, ((1,), (0,)))

        def across():
            h, m, l = split3(hdot(inv, work[rows, :npad], ((1,), (0,))))
            for q, part in enumerate((h, m, h, m, l, h)):
                right[q * B:(q + 1) * B, :npad] = part
            work[rows, :] = jnp.zeros((B, wid), F32)
            work[rows, rows] = jnp.where(r0 == r1, 1.0, 0.0).astype(F32)

        def down():
            h, m, l = split3(spread(j, rows, inv, diag))
            for q, part in enumerate((h, h, m, m, h, l)):
                left[:, q * B:(q + 1) * B] = part

        def update(q):
            cols = pl.ds(pl.multiple_of(jnp.minimum((j + 1) * B + q * 2 * B, npad), B), 2 * B)
            work[:, cols] = work[:, cols] - jnp.dot(left[...], right[:, cols], preferred_element_type=F32)

        items = [across, down] + [functools.partial(update, q) for q in range(pieces)]
        items.append(functools.partial(gather_up, j, rows))
        factor_inverse(next_diag, linv, items, used)
        return carry

    tail = -(-(rank - (npad - B)) // 8) * 8
    for start in range(first, min(last, nb - 2), 2):
        stop = min(start + 2, last, nb - 2)
        lax.fori_loop(start, stop, functools.partial(step, (nb - start) // 2, B), 0)
    if whole:
        lax.fori_loop(nb - 2, nb - 1, functools.partial(step, 1, tail), 0)
    if not whole:
        work_out[...] = work[:, last * B:npad]
        linv_out[...] = linv[...]
        sum_out[...] = total[...]
        return
    rows = slice(npad - B, npad)
    diag = work[rows, rows]
    work[rows, :] = jnp.zeros((B, wid), F32)
    work[rows, rows] = jnp.where(r0 == r1, 1.0, 0.0).astype(F32)
    spread(nb - 1, rows, linv[...], diag)
    gather_up(None, rows)
    if not whole_l:
        result_ref[...] = total[...].astype(BF)


def factor(operands, results, width, rank, first, last, root_rows=None, root_cols=None):
    nb = width // B
    vmem = pl.BlockSpec(memory_space=pltpu.VMEM)
    scratch = [
        pltpu.VMEM((width, width + 2 * B), F32),
        pltpu.VMEM((B, B), F32),
        pltpu.VMEM((width, 6 * B), BF),
        pltpu.VMEM((6 * B, width + 2 * B), BF),
        pltpu.VMEM((width, 2 * B), BF),
        pltpu.VMEM((width, B), BF),
    ]
    if root_rows is None:
        count = operands[-1].shape[0]
        scratch.append(pltpu.VMEM((count, width), F32))
    return pl.pallas_call(
        functools.partial(factor_kernel, nb, rank, first, last, root_rows, root_cols),
        out_shape=tuple(jax.ShapeDtypeStruct(shape, kind) for shape, kind in results),
        in_specs=[vmem] * len(operands),
        out_specs=(vmem,) * len(results),
        scratch_shapes=scratch,
        compiler_params=pltpu.CompilerParams(vmem_limit_bytes=30 * 1024 * 1024),
        cost_estimate=pl.CostEstimate(flops=20 * width**3, bytes_accessed=200_000_000, transcendentals=0),
    )(*operands)


def two_stage(blocks, rows, width, rank):
    count = rows.shape[0]
    half = 3
    state = factor(
        (blocks, rows), [((width, width - half * B), F32), ((B, B), F32), ((count, width), F32)], width, rank, 0, half)

    def finish(state):
        return factor((*state, rows), [((count, width), BF)], width, rank, half, width // B)[0]

    return state, finish


def per_device(weight, test_matrix, fisher):
    row_count = lax.axis_size("row")
    col_count = lax.axis_size("col")
    col_index = lax.axis_index("col")
    block_rows = weight.shape[0]
    slice_rows = block_rows // col_count
    total_rows = block_rows * row_count
    total_cols = weight.shape[1] * col_count
    rank = test_matrix.shape[1]
    width = -(-rank // B) * B
    scales = jnp.sqrt(fisher)
    own_scales = lax.dynamic_slice_in_dim(scales, col_index * slice_rows, slice_rows, 0)
    sketch, weighted_rows = sketch_rows(weight, test_matrix, own_scales, width, 3)
    weighted = lax.all_gather(weighted_rows, "col", axis=0, tiled=True)
    gram_one = gram_sum(sketch, 1)
    state, finish = two_stage(gram_one, sketch, width, rank)
    weighted, state = lax.optimization_barrier((weighted, state))
    combos = lax.psum_scatter(
        lax.dot_general(
            weighted, weight, (((0,), (0,)), ((), ())), preferred_element_type=F32
        ).astype(BF).T,
        "row",
        scatter_dimension=0,
        tiled=True,
    ).astype(BF)
    projected = finish(state)
    combos, projected = lax.optimization_barrier((combos, projected))
    all_combos = lax.all_gather(combos, "row", axis=0, tiled=True)
    gram_two = gram_sum(combos, 2)
    left_factor, right_turned = factor(
        (gram_two, all_combos, projected, own_scales[:, None]),
        [((slice_rows, rank), BF), ((rank, weight.shape[1]), BF)],
        width, rank, 0, width // B, math.sqrt(total_rows), math.sqrt(total_cols),
    )
    return (left_factor, right_turned.T)


def solution(mesh):
    return jax.shard_map(
        per_device,
        mesh=mesh,
        in_specs=(P("row", "col"), P("col", None), P("row")),
        out_specs=(P(("row", "col"), None), P("col", None)),
        check_vma=False,
    )
```
